128 devices in a mesh: seq: 16 (over x, z), exp: 8 (over y, core).
Axes of the slice: x: 4, y: 4, z: 4, core: 2. Of those that a mesh axis runs over, the one named last changes fastest.
Arguments:
- stream: bfloat16 [8, 2048, 2048], P('exp', 'seq'), may hold values from -6 to 6
- stream_tangent: bfloat16 [8, 2048, 2048], P('exp', 'seq'), may hold values from -6 to 6
- query_rows: bfloat16 [8, 2048, 2048], P('exp', 'seq'), may hold values from -6 to 6
- key_rows: bfloat16 [8, 2048, 2048], P('exp', 'seq'), may hold values from -6 to 6
- value_rows: bfloat16 [8, 2048, 2048], P('exp', 'seq'), may hold values from -6 to 6
- query_tangent: bfloat16 [8, 2048, 2048], P('exp', 'seq'), may hold values from -6 to 6
- key_tangent: bfloat16 [8, 2048, 2048], P('exp', 'seq'), may hold values from -6 to 6
- value_tangent: bfloat16 [8, 2048, 2048], P('exp', 'seq'), may hold values from -6 to 6
- out_proj: bfloat16 [2048, 2048], P('seq'), may hold values from -0.375 to 0.375
- norm_gain: bfloat16 [2048], replicated, may hold values from 0.099609375 to 1.8984375
- gate_weight: bfloat16 [8, 2048, 1408], P('exp'), may hold values from -0.125 to 0.125
- up_weight: bfloat16 [8, 2048, 1408], P('exp'), may hold values from -0.125 to 0.125
- down_weight: bfloat16 [8, 1408, 2048], P('exp'), may hold values from -0.15625 to 0.15625
- route_ids: int32 [8, 2048, 2], P('exp', 'seq'), may hold values from 0 to 7, all different within a row; in each aligned block of 128 rows (0 to 127, 128 to 255, ..., all dimensions but the last counted through in order) at most 64 rows name the same one
- route_weights: bfloat16 [8, 2048, 2], P('exp', 'seq'), may hold values from 0.25 to 1
Outputs:
- layer_out: bfloat16 [8, 2048, 2048], P('exp', 'seq')
- layer_tangent: bfloat16 [8, 2048, 2048], P('exp', 'seq')
The draws below stay inside these ranges and needn't reach their ends.
Inputs may be any that keep to these rules, and one draw needn't show every extreme that they name: `route_ids`: A token's 2 experts differ. Among the 128 tokens of one device (aligned blocks of positions of one sequence), no expert is named more than 64 times, a bound that some block reaches.
All inputs are finite; a program needn't handle non-finite values.
Results may differ from the reference program's by a relative error of at most 0.019.
Values may be sent and summed in bfloat16 or wider, within the bound.
No kernel may reach another device: no remote copies, remote signals or barrier semaphores. Data moves between devices by JAX's collectives and lax.ppermute only.
A program may use at most 192 MiB of HBM per device.

```python
import math
import jax
import jax.numpy as jnp
import numpy as np
from jax import lax

D = 2048
HEADS = 16
HEAD_DIM = 128
FF = 1408
TOPK = 2
TOK_DEV = 128
LEN = 2048
BATCH = 8
TOKENS = 16384
EXPERTS = 8
CAP = 64


def draw_query_rows(key, part):
    key = jax.random.fold_in(key, 3)
    values_drawn = jnp.clip(1.2 * jax.random.normal(key, (BATCH, LEN, D), jnp.float32), -6.0, 6.0)
    return values_drawn.astype(jnp.bfloat16)


def draw_key_rows(key, part):
    key = jax.random.fold_in(key, 5)
    values_drawn = jnp.clip(1.2 * jax.random.normal(key, (BATCH, LEN, D), jnp.float32), -6.0, 6.0)
    return values_drawn.astype(jnp.bfloat16)


def levels(key, dims, pieces, low, high):
    factor_of = 1.0
    for axis_at, blocks in pieces:
        heights = jax.random.uniform(jax.random.fold_in(jax.random.fold_in(key, 6), axis_at), (blocks,), jnp.float32, low / len(pieces), high / len(pieces))
        factor_of = factor_of * jnp.repeat(jnp.exp(heights), dims[axis_at] // blocks).reshape((-1,) + (1,) * (len(dims) - 1 - axis_at))
    return factor_of


def routed_block(rng, own, number, rows, number_of, top, reach, slope):
    sequence = jax.random.permutation(rng, number_of)
    crowded, common = portions_of(number_of, rows * top, reach, slope, True), portions_of(number_of, rows * top, reach, slope, False)
    places = jnp.arange(number_of)

    def named(tallies, offset_by):
        used = int((tallies > 0).sum())
        fixed = max(1, used // 4)
        passed = fixed + (places - fixed + offset_by * (used - fixed)) % max(1, number_of - fixed)
        return jnp.zeros((number_of,), jnp.int32).at[sequence[jnp.where(places < fixed, places, passed)]].set(jnp.asarray(tallies, jnp.int32))

    tallies = jnp.where(number % 4 == 0, named(crowded, number // 4), named(common, number - number // 4 - 1))
    mixed = jax.random.permutation(jax.random.fold_in(own, 3), number_of)
    source_of, sink = mixed[0:number_of // 2 * 2:2], mixed[1:number_of // 2 * 2:2]
    slack = jnp.minimum(tallies[source_of] - 1, reach - tallies[sink]) // 2
    slack = jnp.where((source_of == sequence[0]) | (sink == sequence[0]) | (tallies[sink] == 0), 0, jnp.maximum(slack, 0))
    passed = jax.random.randint(jax.random.fold_in(own, 4), (number_of // 2,), 0, 1 << 20) % (slack + 1)
    tallies = tallies.at[source_of].add(-passed).at[sink].add(passed)
    items = jnp.searchsorted(jnp.cumsum(tallies), jnp.arange(rows * top), side="right").astype(jnp.int32)
    grid = items.reshape(top, rows).T
    grid = grid[jax.random.permutation(jax.random.fold_in(own, 1), rows)]
    offset_by = jax.random.randint(jax.random.fold_in(own, 2), (rows, 1), 0, top)
    return jnp.take_along_axis(grid, (jnp.arange(top)[None, :] + offset_by) % top, axis=1)


def portions_of(number_of, total, bound, skew, full):
    loads = [(1 << 20) // math.isqrt(rank ** skew) + 1 for rank in range(1, number_of + 1)]
    largest = bound if full else min(bound, max(-(-total // number_of), total * loads[0] // sum(loads)))
    least = 1 if total - largest >= number_of - 1 else 0
    holding, spare = [largest] + [least] * (number_of - 1), total - largest - least * (number_of - 1)
    while spare > 0:
        movable = [i for i in range(1, number_of) if holding[i] < largest] or [i for i in range(1, number_of) if holding[i] < bound]
        whole, left = sum([loads[i] for i in movable]), spare
        for i in movable:
            extra = min(bound - holding[i], max(1, left * loads[i] // whole), spare)
            holding[i] = holding[i] + extra
            spare = spare - extra
    return np.array(holding)


def noise(rng, extent, spread, bound, pieces=(), kind=jnp.bfloat16):
    gain = levels(rng, extent, pieces, -0.22, 0.18) if pieces else 1.0
    drawn = jax.random.normal(rng, extent, jnp.float32) * spread * gain
    return jnp.minimum(jnp.maximum(drawn, -bound), bound).astype(kind)


def setup_inputs(seed: int = 0) -> dict:
    streams_of = jax.random.split(jax.random.key(seed), 16)
    stream = noise(streams_of[0], (BATCH, LEN, D), 1.0, 6.0, ((0, 8), (1, 16)))
    stream_tangent = noise(streams_of[1], (BATCH, LEN, D), 1.0, 6.0, ((0, 8), (1, 16)))
    query_rows = draw_query_rows(jax.random.fold_in(streams_of[15], 71), 0)
    key_rows = draw_key_rows(jax.random.fold_in(streams_of[15], 71), 0)
    value_rows = noise(streams_of[4], (BATCH, LEN, D), 1.0, 6.0, ((0, 8), (1, 16)))
    query_tangent = noise(streams_of[5], (BATCH, LEN, D), 1.0, 6.0, ((0, 8), (1, 16)))
    key_tangent = noise(streams_of[6], (BATCH, LEN, D), 1.0, 6.0, ((0, 8), (1, 16)))
    value_tangent = noise(streams_of[7], (BATCH, LEN, D), 1.0, 6.0, ((0, 8), (1, 16)))
    out_proj = noise(streams_of[8], (D, D), (D // 8) ** -0.5, 0.375, ((0, 16),))
    norm_gain = jnp.clip(1.0 + 0.18 * jax.random.normal(streams_of[9], (D,), jnp.float32), 0.099609375, 1.8984375).astype(jnp.bfloat16)
    gate_weight = noise(streams_of[10], (EXPERTS, D, FF), D ** -0.5, 0.125, ((0, 8),))
    up_weight = noise(streams_of[11], (EXPERTS, D, FF), D ** -0.5, 0.125, ((0, 8),))
    down_weight = noise(streams_of[12], (EXPERTS, FF, D), FF ** -0.5, 0.15625, ((0, 8),))
    route_ids_keys = jax.random.split(jax.random.fold_in(streams_of[13], 1), BATCH * LEN // TOK_DEV)
    route_ids_turns = jax.random.permutation(jax.random.fold_in(streams_of[13], 3), BATCH * LEN // TOK_DEV)
    route_ids = jax.vmap(lambda own, number: routed_block(jax.random.fold_in(streams_of[13], 2), own, number, TOK_DEV, EXPERTS, TOPK, CAP, 2))(route_ids_keys, route_ids_turns).reshape((BATCH, LEN, TOPK))
    route_weights = jnp.clip(0.25 + 0.75 * jax.random.uniform(streams_of[14], (BATCH, LEN, TOPK), jnp.float32) ** levels(streams_of[14], (BATCH, LEN, TOPK), ((0, 8), (1, 16)), -0.2, 0.2), 0.25, 1.0).astype(jnp.bfloat16)
    return {"stream": stream, "stream_tangent": stream_tangent, "query_rows": query_rows, "key_rows": key_rows, "value_rows": value_rows, "query_tangent": query_tangent, "key_tangent": key_tangent, "value_tangent": value_tangent, "out_proj": out_proj, "norm_gain": norm_gain, "gate_weight": gate_weight, "up_weight": up_weight, "down_weight": down_weight, "route_ids": route_ids, "route_weights": route_weights}


def head_attention(inputs):
    query_head, key_head, value_head, dquery_head, dkey_head, dvalue_head = inputs
    score_scale = 1.0 / math.sqrt(HEAD_DIM)
    scores = jnp.dot(query_head, key_head.T, preferred_element_type=jnp.float32) * score_scale
    dscores = (jnp.dot(dquery_head, key_head.T, preferred_element_type=jnp.float32) + jnp.dot(query_head, dkey_head.T, preferred_element_type=jnp.float32)) * score_scale
    row_peak = lax.optimization_barrier(jnp.max(scores, axis=-1, keepdims=True))
    exponent = jnp.exp(scores - row_peak)
    row_total = lax.optimization_barrier(jnp.sum(exponent, axis=-1, keepdims=True))
    probability = exponent / row_total
    prob_low = probability.astype(jnp.bfloat16)
    attended = jnp.dot(prob_low, value_head, preferred_element_type=jnp.float32)
    weighted = probability * dscores
    row_sum = lax.optimization_barrier(jnp.sum(weighted, axis=-1, keepdims=True))
    tangent = jnp.dot(weighted.astype(jnp.bfloat16), value_head, preferred_element_type=jnp.float32) + jnp.dot(prob_low, dvalue_head, preferred_element_type=jnp.float32) - row_sum * attended
    return (attended.astype(jnp.bfloat16), tangent.astype(jnp.bfloat16))

def to_heads(array_in):
    return array_in.reshape(BATCH, LEN, HEADS, HEAD_DIM).transpose(0, 2, 1, 3).reshape(BATCH * HEADS, LEN, HEAD_DIM)

def from_heads(array_in):
    return array_in.reshape(BATCH, HEADS, LEN, HEAD_DIM).transpose(0, 2, 1, 3).reshape(TOKENS, D)

def expert_ffn(inputs):
    rows_in, gate_mat, up_mat, down_mat = inputs
    primal_rows = rows_in[:, 0]
    tangent_rows = rows_in[:, 1]
    gate_primal = jnp.dot(primal_rows, gate_mat, preferred_element_type=jnp.float32)
    up_primal = jnp.dot(primal_rows, up_mat, preferred_element_type=jnp.float32)
    gate_tangent = jnp.dot(tangent_rows, gate_mat, preferred_element_type=jnp.float32)
    up_tangent = jnp.dot(tangent_rows, up_mat, preferred_element_type=jnp.float32)
    sigmoid_gate = jax.nn.sigmoid(gate_primal)
    activated = gate_primal * sigmoid_gate
    slope_gate = sigmoid_gate * (1.0 + gate_primal * (1.0 - sigmoid_gate))
    hidden_rows = (activated * up_primal).astype(jnp.bfloat16)
    hidden_tangent = (slope_gate * gate_tangent * up_primal + activated * up_tangent).astype(jnp.bfloat16)
    out_primal = jnp.dot(hidden_rows, down_mat, preferred_element_type=jnp.float32).astype(jnp.bfloat16)
    out_tangent = jnp.dot(hidden_tangent, down_mat, preferred_element_type=jnp.float32).astype(jnp.bfloat16)
    return jnp.stack([out_primal, out_tangent], axis=1)

def reference(stream, stream_tangent, query_rows, key_rows, value_rows, query_tangent, key_tangent, value_tangent, out_proj, norm_gain, gate_weight, up_weight, down_weight, route_ids, route_weights):
    heads_in = tuple((to_heads(array_in) for array_in in (query_rows, key_rows, value_rows, query_tangent, key_tangent, value_tangent)))
    attn_low, attn_tangent = lax.map(head_attention, heads_in)
    attn_low = from_heads(attn_low)
    attn_tangent = from_heads(attn_tangent)
    hidden = stream.reshape(TOKENS, D).astype(jnp.float32) + jnp.dot(attn_low, out_proj, preferred_element_type=jnp.float32)
    hidden_tangent = stream_tangent.reshape(TOKENS, D).astype(jnp.float32) + jnp.dot(attn_tangent, out_proj, preferred_element_type=jnp.float32)
    gain_f = norm_gain.astype(jnp.float32)
    inverse = lax.rsqrt(lax.optimization_barrier(jnp.mean(hidden * hidden, axis=-1, keepdims=True)) + 1e-06)
    cross = lax.optimization_barrier(jnp.mean(hidden * hidden_tangent, axis=-1, keepdims=True))
    normed = (hidden * inverse * gain_f).astype(jnp.bfloat16)
    normed_tangent = (gain_f * (hidden_tangent * inverse - hidden * (inverse * inverse * inverse) * cross)).astype(jnp.bfloat16)
    both_rows = jnp.stack([normed, normed_tangent], axis=1)
    block_count = TOKENS // TOK_DEV
    route_count = TOK_DEV * TOPK
    flat_ids = route_ids.reshape(block_count, route_count).astype(jnp.int32)
    onehot = (flat_ids[:, :, None] == jnp.arange(EXPERTS, dtype=jnp.int32)[None, None, :]).astype(jnp.int32)
    rank_in = lax.optimization_barrier(jnp.sum((jnp.cumsum(onehot, axis=1) - onehot) * onehot, axis=-1)).astype(jnp.int32)
    block_idx = jnp.broadcast_to(jnp.arange(block_count, dtype=jnp.int32)[:, None], (block_count, route_count))
    token_idx = (block_idx * TOK_DEV + jnp.arange(route_count, dtype=jnp.int32)[None, :] // TOPK).astype(jnp.int32)
    buffer_rows = jnp.zeros((EXPERTS, block_count, CAP, 2, D), jnp.bfloat16)
    buffer_rows = buffer_rows.at[flat_ids, block_idx, rank_in].set(both_rows[token_idx])
    results = lax.map(expert_ffn, (buffer_rows.reshape(EXPERTS, block_count * CAP, 2, D), gate_weight, up_weight, down_weight))
    results = results.reshape(EXPERTS, block_count, CAP, 2, D)
    picked = results[flat_ids, block_idx, rank_in].astype(jnp.float32)
    weights_f = route_weights.reshape(block_count, route_count).astype(jnp.float32)
    mixed = lax.optimization_barrier(jnp.sum((picked * weights_f[:, :, None, None]).reshape(TOKENS, TOPK, 2, D), axis=1))
    layer_out = (hidden + mixed[:, 0]).astype(jnp.bfloat16).reshape(BATCH, LEN, D)
    layer_tangent = (hidden_tangent + mixed[:, 1]).astype(jnp.bfloat16).reshape(BATCH, LEN, D)
    return (layer_out, layer_tangent)
```

```python
import functools
import math

import jax
import jax.numpy as jnp
from jax import lax
from jax.experimental import pallas as pl
from jax.experimental.pallas import tpu as pltpu
from jax.sharding import PartitionSpec as P

HEAD_DIM = 128
BF16 = jnp.bfloat16
F32 = jnp.float32
MIB = 2**20


def dot(a, b):
    return jnp.dot(a, b, preferred_element_type=F32)


def pack_kernel(*refs):
    ins, out = refs[:-1], refs[-1]
    heads = out.shape[0]
    for h in range(heads):
        for a, ref in enumerate(ins):
            out[h, a] = ref[:, h * HEAD_DIM : (h + 1) * HEAD_DIM]


def pack(arrays):
    rows, width = arrays[0].shape
    heads = width // HEAD_DIM
    step = 4
    return pl.pallas_call(
        pack_kernel,
        grid=(heads // step,),
        out_shape=jax.ShapeDtypeStruct((heads, len(arrays), rows, HEAD_DIM), BF16),
        in_specs=[pl.BlockSpec((rows, step * HEAD_DIM), lambda i: (0, i))] * len(arrays),
        out_specs=pl.BlockSpec((step, len(arrays), rows, HEAD_DIM), lambda i: (i, 0, 0, 0)),
        cost_estimate=pl.CostEstimate(
            flops=0, bytes_accessed=4 * len(arrays) * rows * width, transcendentals=0
        ),
        name="pack_heads",
    )(*arrays)


def attend_kernel(blocks, r_ref, o_ref, kt, vv):
    sources, _, rows, _ = r_ref.shape
    i = pl.program_id(0)

    @pl.when(i == 0)
    def _():
        for s in range(sources):
            at = slice(s * rows, (s + 1) * rows)
            kt[:HEAD_DIM, at] = r_ref[s, 1].T
            kt[HEAD_DIM:, at] = r_ref[s, 4].T
            vv[at, :HEAD_DIM] = r_ref[s, 2]
            vv[at, HEAD_DIM:] = r_ref[s, 5]

    scale = 1.0 / math.sqrt(HEAD_DIM)
    q = r_ref[pl.ds(i * blocks, blocks), 0].reshape(blocks * rows, HEAD_DIM)
    dq = r_ref[pl.ds(i * blocks, blocks), 3].reshape(blocks * rows, HEAD_DIM)
    s = dot(q, kt[:HEAD_DIM])
    ds = dot(jnp.concatenate([dq, q], axis=1), kt[...])
    m = jnp.max(s, axis=-1, keepdims=True)
    e = jnp.exp2((s - m) * (scale * math.log2(math.e)))
    total = jnp.sum(e, axis=-1, keepdims=True)
    w = e * ds
    row_sum = jnp.sum(w, axis=-1, keepdims=True)
    both = dot(e.astype(BF16), vv[...])
    wv = dot(w.astype(BF16), vv[:, :HEAD_DIM])
    inv = 1.0 / total
    att = both[:, :HEAD_DIM] * inv
    tan = (wv * scale + both[:, HEAD_DIM:]) * inv - (row_sum * (inv * scale)) * att
    o_ref[:, 0] = att.astype(BF16).reshape(blocks, rows, HEAD_DIM)
    o_ref[:, 1] = tan.astype(BF16).reshape(blocks, rows, HEAD_DIM)


def attend(received, blocks=2):
    sources, _, rows, _ = received.shape
    seq_len = sources * rows
    return pl.pallas_call(
        functools.partial(attend_kernel, blocks),
        grid=(sources // blocks,),
        out_shape=jax.ShapeDtypeStruct((sources, 2, rows, HEAD_DIM), BF16),
        in_specs=[pl.BlockSpec(received.shape, lambda i: (0, 0, 0, 0))],
        out_specs=pl.BlockSpec((blocks, 2, rows, HEAD_DIM), lambda i: (i, 0, 0, 0)),
        scratch_shapes=[
            pltpu.VMEM((2 * HEAD_DIM, seq_len), BF16),
            pltpu.VMEM((seq_len, 2 * HEAD_DIM), BF16),
        ],
        compiler_params=pltpu.CompilerParams(vmem_limit_bytes=48 * MIB),
        cost_estimate=pl.CostEstimate(
            flops=16 * seq_len * seq_len * HEAD_DIM,
            bytes_accessed=16 * seq_len * HEAD_DIM,
            transcendentals=seq_len * seq_len,
        ),
        name="attend_head",
    )(received)


def project_kernel(a_ref, w_ref, s_ref, ds_ref, g_ref, h_ref, n_ref, x, acc):
    heads, _, rows, _ = a_ref.shape
    tile = w_ref.shape[2]
    i = pl.program_id(0)

    @pl.when(i == 0)
    def _():
        for h in range(heads):
            at = slice(h * HEAD_DIM, (h + 1) * HEAD_DIM)
            x[:rows, at] = a_ref[h, 0]
            x[rows:, at] = a_ref[h, 1]

    out = dot(x[...], w_ref[0])
    at = pl.ds(pl.multiple_of(i * tile, tile), tile)
    acc[:rows, at] = out[:rows] + s_ref[:, at].astype(F32)
    acc[rows:, at] = out[rows:] + ds_ref[:, at].astype(F32)

    @pl.when(i == pl.num_programs(0) - 1)
    def _():
        hid = acc[:rows, :]
        tan = acc[rows:, :]
        gain = g_ref[...].astype(F32)
        inverse = lax.rsqrt(jnp.mean(hid * hid, axis=-1, keepdims=True) + 1e-06)
        cross = jnp.mean(hid * tan, axis=-1, keepdims=True)
        width = hid.shape[1]
        h_ref[:, :width] = hid
        h_ref[:, width:] = tan
        n_ref[:, :width] = (hid * inverse * gain).astype(BF16)
        n_ref[:, width:] = (
            gain * (tan * inverse - hid * (inverse * inverse * inverse) * cross)
        ).astype(BF16)


def project(attended, weights, stream, stream_tangent, gain):
    tiles, width, tile = weights.shape
    rows = stream.shape[0]
    full = lambda shape: pl.BlockSpec(shape, lambda i: (0,) * len(shape))
    return pl.pallas_call(
        project_kernel,
        grid=(tiles,),
        out_shape=(
            jax.ShapeDtypeStruct((rows, 2 * width), F32),
            jax.ShapeDtypeStruct((rows, 2 * width), BF16),
        ),
        in_specs=[
            full(attended.shape),
            pl.BlockSpec((1, width, tile), lambda i: (i, 0, 0)),
            full(stream.shape),
            full(stream.shape),
            full((1, width)),
        ],
        out_specs=(full((rows, 2 * width)), full((rows, 2 * width))),
        scratch_shapes=[
            pltpu.VMEM((2 * rows, width), BF16),
            pltpu.VMEM((2 * rows, width), F32),
        ],
        compiler_params=pltpu.CompilerParams(vmem_limit_bytes=48 * MIB),
        cost_estimate=pl.CostEstimate(
            flops=4 * rows * width * width, bytes_accessed=3 * width * width, transcendentals=0
        ),
        name="project_norm",
    )(attended, weights, stream, stream_tangent, gain)


def expert_kernel(up_steps, x_ref, g_ref, u_ref, d_ref, o_ref, hid):
    rows = x_ref.shape[0]
    width = x_ref.shape[1] // 2
    tile = g_ref.shape[1]
    i = pl.program_id(0)
    block = 256

    @pl.when(i < up_steps)
    def _():
        at = pl.ds(pl.multiple_of(i * tile, tile), tile)
        weights = jnp.concatenate([g_ref[...], u_ref[...]], axis=1)

        def step(j, carry):
            r = pl.ds(pl.multiple_of(j * block, block), block)
            primal = dot(x_ref[r, :width], weights)
            tangent = dot(x_ref[r, width:], weights)
            gate, up = primal[:, :tile], primal[:, tile:]
            dgate, dup = tangent[:, :tile], tangent[:, tile:]
            sig = jax.nn.sigmoid(gate)
            act = gate * sig
            slope = sig * (1.0 + gate * (1.0 - sig))
            hid[0, r, at] = (act * up).astype(BF16)
            hid[1, r, at] = (slope * dgate * up + act * dup).astype(BF16)
            return carry

        lax.fori_loop(0, rows // block, step, 0, unroll=True)

    @pl.when(i >= up_steps)
    def _():
        def step(j, carry):
            r = pl.ds(pl.multiple_of(j * block, block), block)
            o_ref[0, r] = dot(hid[0, r], d_ref[...]).astype(BF16)
            o_ref[1, r] = dot(hid[1, r], d_ref[...]).astype(BF16)
            return carry

        lax.fori_loop(0, rows // block, step, 0, unroll=True)


def expert(x, gate, up, down):
    rows, both = x.shape
    width, ff = gate.shape
    tile = 128
    up_steps = ff // tile
    cols = 256
    down_steps = width // cols
    return pl.pallas_call(
        functools.partial(expert_kernel, up_steps),
        grid=(up_steps + down_steps,),
        out_shape=jax.ShapeDtypeStruct((2, rows, width), BF16),
        in_specs=[
            pl.BlockSpec((rows, both), lambda i: (0, 0)),
            pl.BlockSpec((width, tile), lambda i: (0, jnp.minimum(i, up_steps - 1))),
            pl.BlockSpec((width, tile), lambda i: (0, jnp.minimum(i, up_steps - 1))),
            pl.BlockSpec((ff, cols), lambda i: (0, jnp.maximum(i - up_steps, 0))),
        ],
        out_specs=pl.BlockSpec((2, rows, cols), lambda i: (0, 0, jnp.maximum(i - up_steps, 0))),
        scratch_shapes=[pltpu.VMEM((2, rows, ff), BF16)],
        compiler_params=pltpu.CompilerParams(vmem_limit_bytes=48 * MIB),
        cost_estimate=pl.CostEstimate(
            flops=12 * rows * width * ff, bytes_accessed=6 * width * ff + 8 * rows * both,
            transcendentals=rows * ff,
        ),
        name="expert_rows",
    )(x, gate, up, down)


def shards(
    stream,
    stream_tangent,
    query_rows,
    key_rows,
    value_rows,
    query_tangent,
    key_tangent,
    value_tangent,
    out_proj,
    norm_gain,
    gate_weight,
    up_weight,
    down_weight,
    route_ids,
    route_weights,
):
    owner_count = lax.axis_size("exp")
    tok_dev, width = stream.shape[1:]
    own = lax.axis_index("exp")

    cols = width // owner_count
    own_cols = lax.dynamic_slice_in_dim(out_proj, own * cols, cols, axis=1)
    own_cols = lax.all_gather(own_cols, "seq", axis=0, tiled=True)
    weights = lax.all_gather(own_cols, "exp", axis=0, tiled=False)

    sent = pack(
        [
            query_rows[0],
            key_rows[0],
            value_rows[0],
            query_tangent[0],
            key_tangent[0],
            value_tangent[0],
        ]
    )
    received = lax.all_to_all(sent, "seq", split_axis=0, concat_axis=0, tiled=True)
    attended = attend(received)
    returned = lax.all_to_all(attended, "seq", split_axis=0, concat_axis=0, tiled=True)
    hidden, normed = project(
        returned, weights, stream[0], stream_tangent[0], norm_gain.reshape(1, -1)
    )

    topk_count = route_ids.shape[2]
    experts_total = owner_count * gate_weight.shape[0]
    capacity = 2 * tok_dev * topk_count // experts_total
    flat_ids = route_ids.reshape(-1)
    onehot = (flat_ids[:, None] == jnp.arange(experts_total, dtype=jnp.int32)[None, :]).astype(
        jnp.int32
    )
    rank_in = jnp.sum((jnp.cumsum(onehot, axis=0) - onehot) * onehot, axis=1)
    slot_ids = (flat_ids * capacity + rank_in).reshape(tok_dev, topk_count)
    slot_index = jnp.arange(experts_total * capacity, dtype=jnp.int32)
    slot_hits = slot_ids[None, :, :] == slot_index[:, None, None]
    dispatch_matrix = jnp.sum(slot_hits.astype(jnp.int32), axis=-1).astype(BF16)
    combine_matrix = jnp.sum(
        jnp.where(slot_hits, route_weights[0][None, :, :], 0.0).astype(F32), axis=-1
    ).astype(BF16)

    send_rows = dot(dispatch_matrix, normed).astype(BF16)
    send_rows = send_rows.reshape(owner_count, capacity, 2 * width)
    arrived = lax.all_to_all(send_rows, "exp", split_axis=0, concat_axis=0, tiled=True)
    processed = expert(
        arrived.reshape(owner_count * capacity, 2 * width),
        gate_weight[0],
        up_weight[0],
        down_weight[0],
    )
    processed = processed.reshape(2, owner_count, capacity, width)
    results = lax.all_to_all(processed, "exp", split_axis=1, concat_axis=1, tiled=True)
    results = results.reshape(2, experts_total * capacity, width)
    mixed = jnp.einsum("st,psd->ptd", combine_matrix, results, preferred_element_type=F32)
    layer_out = (hidden[:, :width] + mixed[0]).astype(BF16)[None]
    layer_tangent = (hidden[:, width:] + mixed[1]).astype(BF16)[None]
    return (layer_out, layer_tangent)


def solution(mesh):
    rows = P("exp", "seq", None)
    in_specs = (rows,) * 8 + (
        P("seq", None),
        P(),
        P("exp", None, None),
        P("exp", None, None),
        P("exp", None, None),
        rows,
        rows,
    )
    return jax.shard_map(
        shards, mesh=mesh, in_specs=in_specs, out_specs=(rows, rows), check_vma=False
    )
```

```python
import functools
import math

import jax
import jax.numpy as jnp
from jax import lax
from jax.experimental import pallas as pl
from jax.experimental.pallas import tpu as pltpu
from jax.sharding import PartitionSpec as P

HEAD_DIM = 128
BF16 = jnp.bfloat16
F32 = jnp.float32
MIB = 2**20


def dot(a, b):
    return jnp.dot(a, b, preferred_element_type=F32)


def pack_kernel(*refs):
    ins, out = refs[:-1], refs[-1]
    heads = out.shape[0]
    for h in range(heads):
        for a, ref in enumerate(ins):
            out[h, a] = ref[:, h * HEAD_DIM : (h + 1) * HEAD_DIM]


def pack(arrays):
    rows, width = arrays[0].shape
    heads = width // HEAD_DIM
    step = 4
    return pl.pallas_call(
        pack_kernel,
        grid=(heads // step,),
        out_shape=jax.ShapeDtypeStruct((heads, len(arrays), rows, HEAD_DIM), BF16),
        in_specs=[pl.BlockSpec((rows, step * HEAD_DIM), lambda i: (0, i))] * len(arrays),
        out_specs=pl.BlockSpec((step, len(arrays), rows, HEAD_DIM), lambda i: (i, 0, 0, 0)),
        cost_estimate=pl.CostEstimate(
            flops=0, bytes_accessed=4 * len(arrays) * rows * width, transcendentals=0
        ),
        name="pack_heads",
    )(*arrays)


def attend_kernel(blocks, r_ref, o_ref, t_ref, kt, vv):
    sources, _, rows, _ = r_ref.shape
    i = pl.program_id(0)

    @pl.when(i == 0)
    def _():
        for s in range(sources):
            at = slice(s * rows, (s + 1) * rows)
            kt[:HEAD_DIM, at] = r_ref[s, 1].T
            kt[HEAD_DIM:, at] = r_ref[s, 4].T
            vv[at, :HEAD_DIM] = r_ref[s, 2]
            vv[at, HEAD_DIM:] = r_ref[s, 5]

    scale = 1.0 / math.sqrt(HEAD_DIM)
    q = r_ref[pl.ds(i * blocks, blocks), 0].reshape(blocks * rows, HEAD_DIM)
    dq = r_ref[pl.ds(i * blocks, blocks), 3].reshape(blocks * rows, HEAD_DIM)
    s = dot(q, kt[:HEAD_DIM])
    ds = dot(jnp.concatenate([dq, q], axis=1), kt[...])
    m = jnp.max(s, axis=-1, keepdims=True)
    e = jnp.exp2((s - m) * (scale * math.log2(math.e)))
    total = jnp.sum(e, axis=-1, keepdims=True)
    w = e * ds
    row_sum = jnp.sum(w, axis=-1, keepdims=True)
    both = dot(e.astype(BF16), vv[...])
    wv = dot(w.astype(BF16), vv[:, :HEAD_DIM])
    inv = 1.0 / total
    att = both[:, :HEAD_DIM] * inv
    tan = (wv * scale + both[:, HEAD_DIM:]) * inv - (row_sum * (inv * scale)) * att
    o_ref[...] = att.astype(BF16).reshape(blocks, rows, HEAD_DIM)
    t_ref[...] = tan.astype(BF16).reshape(blocks, rows, HEAD_DIM)


def attend(received, blocks=2):
    sources, _, rows, _ = received.shape
    seq_len = sources * rows
    shape = jax.ShapeDtypeStruct((sources, rows, HEAD_DIM), BF16)
    spec = pl.BlockSpec((blocks, rows, HEAD_DIM), lambda i: (i, 0, 0))
    return pl.pallas_call(
        functools.partial(attend_kernel, blocks),
        grid=(sources // blocks,),
        out_shape=(shape, shape),
        in_specs=[pl.BlockSpec(received.shape, lambda i: (0, 0, 0, 0))],
        out_specs=(spec, spec),
        scratch_shapes=[
            pltpu.VMEM((2 * HEAD_DIM, seq_len), BF16),
            pltpu.VMEM((seq_len, 2 * HEAD_DIM), BF16),
        ],
        compiler_params=pltpu.CompilerParams(vmem_limit_bytes=48 * MIB),
        cost_estimate=pl.CostEstimate(
            flops=16 * seq_len * seq_len * HEAD_DIM,
            bytes_accessed=16 * seq_len * HEAD_DIM,
            transcendentals=seq_len * seq_len,
        ),
        name="attend_head",
    )(received)


def accumulate(order, a_ref, w_refs, s_ref, acc, x):
    heads = a_ref.shape[0]
    for h in range(heads):
        x[:, h * HEAD_DIM : (h + 1) * HEAD_DIM] = a_ref[h]
    half = x.shape[1] // 2
    width = w_refs[0].shape[1]
    tile = 256
    for n in range(4):
        for c in range(0, width, tile):
            if n < 3:
                out = dot(x[...], w_refs[n][:, c : c + tile])
            else:
                out = dot(x[:, :half], w_refs[3][:half, c : c + tile]) + dot(
                    x[:, half:], w_refs[3][half:, c : c + tile]
                )
            at = pl.ds(pl.multiple_of(order[n] * width + c, tile), tile)
            acc[:, at] = out + s_ref[:, at].astype(F32)


def primal_kernel(order, a_ref, w0, w1, w2, w3, s_ref, g_ref, i_ref, h_ref, m_ref, x):
    accumulate(order, a_ref, (w0, w1, w2, w3), s_ref, h_ref, x)
    hid = h_ref[...]
    inverse = lax.rsqrt(jnp.mean(hid * hid, axis=-1, keepdims=True) + 1e-06)
    normed = (hid * inverse * g_ref[...].astype(F32)).astype(BF16)
    half = hid.shape[0] // 2
    info = i_ref.shape[0]
    m_ref[:half] = normed[:half]
    m_ref[half : half + info] = jnp.zeros((info, hid.shape[1]), BF16)
    m_ref[half : half + info, : i_ref.shape[1]] = i_ref[...]
    m_ref[half + info :] = normed[half:]


def tangent_kernel(order, a_ref, w0, w1, w2, w3, s_ref, g_ref, hid_ref, h_ref, m_ref, x):
    accumulate(order, a_ref, (w0, w1, w2, w3), s_ref, h_ref, x)
    hid = hid_ref[...]
    tan = h_ref[...]
    inverse = lax.rsqrt(jnp.mean(hid * hid, axis=-1, keepdims=True) + 1e-06)
    cross = jnp.mean(hid * tan, axis=-1, keepdims=True)
    m_ref[...] = (
        g_ref[...].astype(F32)
        * (tan * inverse - hid * (inverse * inverse * inverse) * cross)
    ).astype(BF16)


def project(kernel, order, attended, weights, stream, gain, extra, sent_rows):
    rows, width = stream.shape
    vmem = pl.BlockSpec(memory_space=pltpu.VMEM)
    return pl.pallas_call(
        kernel,
        out_shape=(
            jax.ShapeDtypeStruct((rows, width), F32),
            jax.ShapeDtypeStruct((sent_rows, width), BF16),
        ),
        in_specs=[pl.BlockSpec(memory_space=pltpu.SMEM)] + [vmem] * 8,
        out_specs=(vmem, vmem),
        scratch_shapes=[pltpu.VMEM((rows, width), BF16)],
        compiler_params=pltpu.CompilerParams(vmem_limit_bytes=48 * MIB),
        cost_estimate=pl.CostEstimate(
            flops=2 * rows * width * width, bytes_accessed=3 * width * width, transcendentals=0
        ),
        name="project_norm",
    )(order, attended, *weights, stream, gain, extra)


SLOTS = 64
INFO = 16
TILE = 128
COLS = 256


def expert_kernel(primal, rows, *refs):
    it = iter(refs)
    take = lambda n: [next(it) for _ in range(n)]
    (me,) = take(1)
    messages = take(8)
    gate, up, down = take(3)
    if primal:
        own, other, coef, disp, comb = take(5)
    else:
        coef_in, disp, comb = take(3)
        own, other = take(2)
    mb, wb, db, xs, hid, ct, msem, wsem, dsem = take(9)
    tokens, width = own.shape[1:]
    ff = gate.shape[1]
    x, s0, fp, fm, s1, f1, f2, s2 = messages
    cut = f1.shape[0]
    pieces = [
        (x, mb.at[0]),
        (s0, mb.at[1]),
        (fp, mb.at[2]),
        (s1.at[:rows], mb.at[3]),
        (fm, mb.at[4]),
        (s1.at[rows:], mb.at[5]),
        (f1, mb.at[6, :cut]),
        (f2, mb.at[6, cut:]),
        (s2, mb.at[7]),
    ]
    loads = [pltpu.make_async_copy(a, b, msem.at[n]) for n, (a, b) in enumerate(pieces)]
    for load in loads:
        load.start()

    def up_loads(f):
        at = pl.ds(pl.multiple_of(f * TILE, TILE), TILE)
        return (
            pltpu.make_async_copy(gate.at[:, at], wb.at[f, :, :TILE], wsem.at[0, f]),
            pltpu.make_async_copy(up.at[:, at], wb.at[f, :, TILE:], wsem.at[1, f]),
        )

    def down_load(j):
        at = pl.ds(pl.multiple_of(j * COLS, COLS), COLS)
        return pltpu.make_async_copy(down.at[:, at], db.at[j], dsem.at[j])

    for f in range(ff // TILE):
        for load in up_loads(f):
            load.start()
    for j in range(width // COLS):
        down_load(j).start()
    for load in loads:
        load.wait()

    for k in range(8):
        if primal:
            half = tokens // 2
            info = mb[k, half : half + INFO, :tokens].astype(F32)
            slot = lax.broadcasted_iota(jnp.int32, (SLOTS, tokens), 0).astype(F32)
            mine = me[0].astype(F32)
            d = jnp.zeros((SLOTS, tokens), F32)
            c = jnp.zeros((SLOTS, tokens), F32)
            for n in range(2):
                hit = (info[3 * n : 3 * n + 1] == mine) & (info[3 * n + 1 : 3 * n + 2] == slot)
                d = d + jnp.where(hit, 1.0, 0.0)
                c = c + jnp.where(hit, info[3 * n + 2 : 3 * n + 3], 0.0)
            disp[k] = d.astype(BF16)
            comb[k] = c.astype(BF16)
            ct[k] = c.T.astype(BF16)
            tok = jnp.concatenate([mb[k, :half], mb[k, half + INFO :]], axis=0)
        else:
            ct[k] = comb[k].astype(F32).T.astype(BF16)
            tok = mb[k]
        xs[k * SLOTS : (k + 1) * SLOTS] = dot(disp[k], tok).astype(BF16)

    def up_step(f, carry):
        for load in up_loads(f):
            load.wait()
        at = pl.ds(pl.multiple_of(f * TILE, TILE), TILE)
        both = dot(xs[...], wb[f])
        g, u = both[:, :TILE], both[:, TILE:]
        if primal:
            sig = jax.nn.sigmoid(g)
            act = g * sig
            hid[:, at] = (act * u).astype(BF16)
            coef[0, :, at] = (sig * (1.0 + g * (1.0 - sig)) * u).astype(BF16)
            coef[1, :, at] = act.astype(BF16)
        else:
            hid[:, at] = (
                coef_in[0, :, at].astype(F32) * g + coef_in[1, :, at].astype(F32) * u
            ).astype(BF16)
        return carry

    lax.fori_loop(0, ff // TILE, up_step, 0)

    def down_step(j, carry):
        down_load(j).wait()
        at = pl.ds(pl.multiple_of(j * COLS, COLS), COLS)
        out = dot(hid[...], db[j]).astype(BF16)
        for k in range(8):
            part = dot(ct[k], out[k * SLOTS : (k + 1) * SLOTS]).astype(BF16)
            (own, other)[k % 2][k // 2, :, at] = part
        return carry

    lax.fori_loop(0, width // COLS, down_step, 0)


def expert(primal, me, messages, weights, more):
    gate, up, down = weights
    width, ff = gate.shape
    tokens = more[1].shape[2] if more else messages[0].shape[0] - INFO
    rows = messages[0].shape[0]
    slots = 8 * SLOTS
    vmem = pl.BlockSpec(memory_space=pltpu.VMEM)
    anywhere = pl.BlockSpec(memory_space=pl.ANY)
    out_shape = [jax.ShapeDtypeStruct((4, tokens, width), BF16)] * 2
    if primal:
        out_shape += [
            jax.ShapeDtypeStruct((2, slots, ff), BF16),
            jax.ShapeDtypeStruct((8, SLOTS, tokens), BF16),
            jax.ShapeDtypeStruct((8, SLOTS, tokens), BF16),
        ]
    return pl.pallas_call(
        functools.partial(expert_kernel, primal, rows),
        out_shape=tuple(out_shape),
        in_specs=[pl.BlockSpec(memory_space=pltpu.SMEM)]
        + [anywhere] * 11
        + [vmem] * len(more),
        out_specs=(vmem,) * len(out_shape),
        scratch_shapes=[
            pltpu.VMEM((8, rows, width), BF16),
            pltpu.VMEM((ff // TILE, width, 2 * TILE), BF16),
            pltpu.VMEM((width // COLS, ff, COLS), BF16),
            pltpu.VMEM((slots, width), BF16),
            pltpu.VMEM((slots, ff), BF16),
            pltpu.VMEM((8, tokens, SLOTS), BF16),
            pltpu.SemaphoreType.DMA((9,)),
            pltpu.SemaphoreType.DMA((2, ff // TILE)),
            pltpu.SemaphoreType.DMA((width // COLS,)),
        ],
        compiler_params=pltpu.CompilerParams(vmem_limit_bytes=56 * MIB),
        cost_estimate=pl.CostEstimate(
            flops=6 * slots * width * ff,
            bytes_accessed=6 * width * ff + 24 * tokens * width,
            transcendentals=slots * ff,
        ),
        name="expert_primal" if primal else "expert_tangent",
    )(me, *messages, gate, up, down, *more)


def step_y(x, distance):
    chips = lax.axis_size("exp") // 2
    pairs = [
        (2 * y + c, 2 * ((y + distance) % chips) + c) for y in range(chips) for c in range(2)
    ]
    return lax.ppermute(x, "exp", pairs)


def swap(x):
    count = lax.axis_size("exp")
    return lax.ppermute(x, "exp", [(n, n ^ 1) for n in range(count)])


def gather_tokens(x, cut):
    s0 = swap(x)
    fp = step_y(x, 1)
    fm = step_y(x, -1)
    f1 = step_y(fp[:cut], 1)
    f2 = step_y(fm[cut:], -1)
    s1 = swap(jnp.concatenate([fp, fm], axis=0))
    s2 = swap(jnp.concatenate([f1, f2], axis=0))
    return [x, s0, fp, fm, s1, f1, f2, s2]


def reduce_tokens(base, own, other):
    got = swap(other)
    both = lambda n: own[n].astype(F32) + got[n].astype(F32)
    half = own.shape[1] // 2
    far = both(3).astype(BF16)
    r1 = step_y(far[:half], 1)
    r2 = step_y(far[half:], -1)
    after, before = both(2), both(1)
    ahead = jnp.concatenate([after[:half] + r1.astype(F32), after[half:]], axis=0).astype(BF16)
    back = jnp.concatenate([before[:half], before[half:] + r2.astype(F32)], axis=0).astype(BF16)
    r3 = step_y(ahead, 1)
    r4 = step_y(back, -1)
    mixed = both(0) + r3.astype(F32) + r4.astype(F32)
    return (base + mixed).astype(BF16)


def gather_projection(out_proj, own):
    y, core = own // 2, own % 2
    width = out_proj.shape[1]
    quarter = width // 4
    mine = (y % 2) * 2 + core
    part = lax.dynamic_slice_in_dim(out_proj, mine * quarter, quarter, axis=1)
    w0 = lax.all_gather(part, "seq", axis=0, tiled=True)
    half = w0.shape[0] // 2
    w1 = swap(w0)
    g1 = step_y(w0[:half], 1)
    g2 = step_y(w0[half:], -1)
    w2 = jnp.concatenate([g1, g2], axis=0)
    w3 = swap(w2)
    order = jnp.stack([mine, mine ^ 1, mine ^ 2, mine ^ 3]).astype(jnp.int32)
    return order, (w0, w1, w2, w3)


def shards(
    stream,
    stream_tangent,
    query_rows,
    key_rows,
    value_rows,
    query_tangent,
    key_tangent,
    value_tangent,
    out_proj,
    norm_gain,
    gate_weight,
    up_weight,
    down_weight,
    route_ids,
    route_weights,
):
    tok_dev = stream.shape[1]
    own = lax.axis_index("exp")
    order, weights = gather_projection(out_proj, own)

    sent = pack(
        [
            query_rows[0],
            key_rows[0],
            value_rows[0],
            query_tangent[0],
            key_tangent[0],
            value_tangent[0],
        ]
    )
    received = lax.all_to_all(sent, "seq", split_axis=0, concat_axis=0, tiled=True)
    attended, attended_tangent = attend(received)
    back = lax.all_to_all(attended, "seq", split_axis=0, concat_axis=0, tiled=True)
    back_tangent = lax.all_to_all(
        attended_tangent, "seq", split_axis=0, concat_axis=0, tiled=True
    )

    experts_total = lax.axis_size("exp")
    flat_ids = route_ids.reshape(-1)
    onehot = (flat_ids[:, None] == jnp.arange(experts_total, dtype=jnp.int32)[None, :]).astype(
        jnp.int32
    )
    rank_in = jnp.sum((jnp.cumsum(onehot, axis=0) - onehot) * onehot, axis=1)
    rank_in = rank_in.reshape(tok_dev, -1)
    ids = route_ids[0]
    fields = []
    for n in range(2):
        fields += [ids[:, n].astype(BF16), rank_in[:, n].astype(BF16), route_weights[0, :, n]]
    info = jnp.concatenate(
        [jnp.stack(fields), jnp.zeros((INFO - len(fields), tok_dev), BF16)], axis=0
    )

    gain = norm_gain.reshape(1, -1)
    hidden, message = project(
        primal_kernel, order, back, weights, stream[0], gain, info, tok_dev + INFO
    )
    hidden_tangent, message_tangent = project(
        tangent_kernel, order, back_tangent, weights, stream_tangent[0], gain, hidden, tok_dev
    )

    me = own.astype(jnp.int32).reshape(1)
    mats = (gate_weight[0], up_weight[0], down_weight[0])
    half = tok_dev // 2
    tokens = gather_tokens(message, half + INFO)
    tokens_tangent = gather_tokens(message_tangent, half)
    part, part_other, *more = expert(True, me, tokens, mats, [])
    dpart, dpart_other = expert(False, me, tokens_tangent, mats, more)
    layer_out = reduce_tokens(hidden, part, part_other)
    layer_tangent = reduce_tokens(hidden_tangent, dpart, dpart_other)
    return (layer_out[None], layer_tangent[None])


def solution(mesh):
    rows = P("exp", "seq", None)
    in_specs = (rows,) * 8 + (
        P("seq", None),
        P(),
        P("exp", None, None),
        P("exp", None, None),
        P("exp", None, None),
        rows,
        rows,
    )
    return jax.shard_map(
        shards, mesh=mesh, in_specs=in_specs, out_specs=(rows, rows), check_vma=False
    )
```

```python
import functools
import math

import jax
import jax.numpy as jnp
import numpy as np
from jax import lax
from jax.experimental import pallas as pl
from jax.experimental.pallas import tpu as pltpu
from jax.sharding import PartitionSpec as P

HEAD_DIM = 128
BF16 = jnp.bfloat16
F32 = jnp.float32
MIB = 2**20


def dot(a, b):
    return jnp.dot(a, b, preferred_element_type=F32)


def pack_kernel(*refs):
    ins, out = refs[:-1], refs[-1]
    heads = out.shape[0]
    for h in range(heads):
        for a, ref in enumerate(ins):
            out[h, a] = ref[:, h * HEAD_DIM : (h + 1) * HEAD_DIM]


def pack(arrays):
    rows, width = arrays[0].shape
    heads = width // HEAD_DIM
    step = 4
    return pl.pallas_call(
        pack_kernel,
        grid=(heads // step,),
        out_shape=jax.ShapeDtypeStruct((heads, len(arrays), rows, HEAD_DIM), BF16),
        in_specs=[pl.BlockSpec((rows, step * HEAD_DIM), lambda i: (0, i))] * len(arrays),
        out_specs=pl.BlockSpec((step, len(arrays), rows, HEAD_DIM), lambda i: (i, 0, 0, 0)),
        cost_estimate=pl.CostEstimate(
            flops=0, bytes_accessed=4 * len(arrays) * rows * width, transcendentals=0
        ),
        name="pack_heads",
    )(*arrays)


def attend_kernel(blocks, r_ref, o_ref, kt, vv):
    sources, _, rows, _ = r_ref.shape
    i = pl.program_id(0)

    @pl.when(i == 0)
    def _():
        for s in range(sources):
            at = slice(s * rows, (s + 1) * rows)
            kt[:HEAD_DIM, at] = r_ref[s, 1].T
            kt[HEAD_DIM:, at] = r_ref[s, 4].T
            vv[at, :HEAD_DIM] = r_ref[s, 2]
            vv[at, HEAD_DIM:] = r_ref[s, 5]

    scale = 1.0 / math.sqrt(HEAD_DIM)
    q = r_ref[pl.ds(i * blocks, blocks), 0].reshape(blocks * rows, HEAD_DIM)
    dq = r_ref[pl.ds(i * blocks, blocks), 3].reshape(blocks * rows, HEAD_DIM)
    s = dot(q, kt[:HEAD_DIM])
    ds = dot(jnp.concatenate([dq, q], axis=1), kt[...])
    m = jnp.max(s, axis=-1, keepdims=True)
    e = jnp.exp2((s - m) * (scale * math.log2(math.e)))
    total = jnp.sum(e, axis=-1, keepdims=True)
    w = e * ds
    row_sum = jnp.sum(w, axis=-1, keepdims=True)
    both = dot(e.astype(BF16), vv[...])
    wv = dot(w.astype(BF16), vv[:, :HEAD_DIM])
    inv = 1.0 / total
    att = both[:, :HEAD_DIM] * inv
    tan = (wv * scale + both[:, HEAD_DIM:]) * inv - (row_sum * (inv * scale)) * att
    o_ref[:, 0] = att.astype(BF16).reshape(blocks, rows, HEAD_DIM)
    o_ref[:, 1] = tan.astype(BF16).reshape(blocks, rows, HEAD_DIM)


def attend(received, blocks=2):
    sources, _, rows, _ = received.shape
    seq_len = sources * rows
    return pl.pallas_call(
        functools.partial(attend_kernel, blocks),
        grid=(sources // blocks,),
        out_shape=jax.ShapeDtypeStruct((sources, 2, rows, HEAD_DIM), BF16),
        in_specs=[pl.BlockSpec(received.shape, lambda i: (0, 0, 0, 0))],
        out_specs=pl.BlockSpec((blocks, 2, rows, HEAD_DIM), lambda i: (i, 0, 0, 0)),
        scratch_shapes=[
            pltpu.VMEM((2 * HEAD_DIM, seq_len), BF16),
            pltpu.VMEM((seq_len, 2 * HEAD_DIM), BF16),
        ],
        compiler_params=pltpu.CompilerParams(vmem_limit_bytes=32 * MIB),
        cost_estimate=pl.CostEstimate(
            flops=16 * seq_len * seq_len * HEAD_DIM,
            bytes_accessed=16 * seq_len * HEAD_DIM,
            transcendentals=seq_len * seq_len,
        ),
        name="attend_head",
    )(received)


def project_kernel(heads, a_ref, *refs):
    w_refs, refs = refs[:8], refs[8:]
    s_ref, t_ref, g_ref, i_ref, h_ref, ht_ref, m_ref, mt_ref, x, wv, sem = refs
    rows, width = h_ref.shape
    deep = width // 8
    loads = [
        pltpu.make_async_copy(ref, wv.at[n * deep : (n + 1) * deep], sem.at[n])
        for n, ref in enumerate(w_refs)
    ]
    for load in loads:
        load.start()
    for h in range(a_ref.shape[0]):
        at = slice(h * HEAD_DIM, (h + 1) * HEAD_DIM)
        x[:rows, at] = a_ref[heads[h], 0]
        x[rows:, at] = a_ref[heads[h], 1]
    half, tile = width // 2, 512
    for part in range(2):
        for load in loads[4 * part : 4 * part + 4]:
            load.wait()
        k = slice(part * half, (part + 1) * half)
        for n in range(0, width, tile):
            at = slice(n, n + tile)
            out = dot(x[:, k], wv[k, at])
            if part == 0:
                h_ref[:, at] = out[:rows] + s_ref[:, at].astype(F32)
                ht_ref[:, at] = out[rows:] + t_ref[:, at].astype(F32)
            else:
                h_ref[:, at] = h_ref[:, at] + out[:rows]
                ht_ref[:, at] = ht_ref[:, at] + out[rows:]
    hid, tan, gain = h_ref[...], ht_ref[...], g_ref[...].astype(F32)
    inverse = lax.rsqrt(jnp.mean(hid * hid, axis=-1, keepdims=True) + 1e-06)
    cross = jnp.mean(hid * tan, axis=-1, keepdims=True)
    normed = (hid * inverse * gain).astype(BF16)
    middle, info = rows // 2, i_ref.shape[0]
    m_ref[:middle] = normed[:middle]
    m_ref[middle : middle + info] = jnp.zeros((info, width), BF16)
    m_ref[middle : middle + info, : i_ref.shape[1]] = i_ref[...]
    m_ref[middle + info :] = normed[middle:]
    mt_ref[...] = (
        gain * (tan * inverse - hid * (inverse * inverse * inverse) * cross)
    ).astype(BF16)


def project(heads, attended, weights, stream, stream_tangent, gain, info):
    rows, width = stream.shape
    vmem = pl.BlockSpec(memory_space=pltpu.VMEM)
    return pl.pallas_call(
        project_kernel,
        out_shape=(
            jax.ShapeDtypeStruct((rows, width), F32),
            jax.ShapeDtypeStruct((rows, width), F32),
            jax.ShapeDtypeStruct((rows + info.shape[0], width), BF16),
            jax.ShapeDtypeStruct((rows, width), BF16),
        ),
        in_specs=[pl.BlockSpec(memory_space=pltpu.SMEM), vmem]
        + [pl.BlockSpec(memory_space=pl.ANY)] * 8
        + [vmem] * 4,
        out_specs=(vmem,) * 4,
        scratch_shapes=[
            pltpu.VMEM((2 * rows, width), BF16),
            pltpu.VMEM((width, width), BF16),
            pltpu.SemaphoreType.DMA((8,)),
        ],
        compiler_params=pltpu.CompilerParams(vmem_limit_bytes=32 * MIB),
        cost_estimate=pl.CostEstimate(
            flops=4 * rows * width * width, bytes_accessed=3 * width * width, transcendentals=0
        ),
        name="project_norm",
    )(heads, attended, *weights, stream, stream_tangent, gain, info)


SLOTS = 64
INFO = 16
TILES = (512, 512, 384)
COLS = 1024


def expert_kernel(primal, rows, *refs):
    it = iter(refs)
    take = lambda n: [next(it) for _ in range(n)]
    (me,) = take(1)
    messages = take(8)
    gate, up, down = take(3)
    if primal:
        own, other, coef, disp, comb = take(5)
    else:
        coef_in, disp, comb = take(3)
        own, other = take(2)
    mb, wb, db, xs, hid, ct, ob, msem, wsem, dsem, osem = take(11)
    if primal:
        cb, csem = take(2)
    tokens, width = own.shape[1:]
    steps, cols = len(TILES), width // COLS
    starts = [sum(TILES[:n]) for n in range(steps)]
    loads = [pltpu.make_async_copy(a, b, msem.at[n]) for n, (a, b) in enumerate(zip(messages, [mb.at[k] for k in range(8)]))]
    for load in loads:
        load.start()

    def up_loads(f):
        at, tile = slice(starts[f], starts[f] + TILES[f]), TILES[f]
        return (
            pltpu.make_async_copy(gate.at[:, at], wb.at[f, :, :tile], wsem.at[0, f]),
            pltpu.make_async_copy(up.at[:, at], wb.at[f, :, tile : 2 * tile], wsem.at[1, f]),
        )

    def down_load(j):
        at = slice(j * COLS, (j + 1) * COLS)
        return pltpu.make_async_copy(down.at[:, at], db.at[j], dsem.at[j])

    for load in up_loads(0):
        load.start()
    ct[...] = jnp.zeros(ct.shape, BF16)
    for load in loads:
        load.wait()
    for load in up_loads(1):
        load.start()

    half = tokens // 2
    none = jnp.zeros((SLOTS, tokens), F32)

    def diagonal(first, second):
        return jnp.concatenate(
            [
                jnp.concatenate([first, none], axis=1),
                jnp.concatenate([none, second], axis=1),
            ],
            axis=0,
        )

    def slots_of(k):
        if not primal:
            return disp[k].astype(F32), comb[k].astype(F32), mb[k]
        info = mb[k, half : half + INFO, :tokens].astype(F32)
        slot = lax.broadcasted_iota(jnp.int32, (SLOTS, tokens), 0).astype(F32)
        mine = me[0].astype(F32)
        d, c = none, none
        for n in range(2):
            hit = (info[3 * n : 3 * n + 1] == mine) & (info[3 * n + 1 : 3 * n + 2] == slot)
            d = d + jnp.where(hit, 1.0, 0.0)
            c = c + jnp.where(hit, info[3 * n + 2 : 3 * n + 3], 0.0)
        disp[k] = d.astype(BF16)
        comb[k] = c.astype(BF16)
        return d, c, jnp.concatenate([mb[k, :half], mb[k, half + INFO :]], axis=0)

    def pair_step(p, carry):
        d0, c0, tok0 = slots_of(2 * p)
        d1, c1, tok1 = slots_of(2 * p + 1)
        q = p % 2
        rows_at = pl.ds(pl.multiple_of(q * 2 * tokens, 2 * tokens), 2 * tokens)
        cols_at = pl.ds(pl.multiple_of(q * 2 * SLOTS, 2 * SLOTS), 2 * SLOTS)
        ct[p // 2, rows_at, cols_at] = diagonal(c0, c1).T.astype(BF16)
        at = pl.ds(pl.multiple_of(p * 2 * SLOTS, 2 * SLOTS), 2 * SLOTS)
        xs[at] = dot(
            diagonal(d0, d1).astype(BF16), jnp.concatenate([tok0, tok1], axis=0)
        ).astype(BF16)
        return carry

    lax.fori_loop(0, 4, pair_step, 0)

    def finish(f, both):
        tile = TILES[f]
        at = slice(starts[f], starts[f] + tile)
        g, u = both[:, :tile], both[:, tile:]
        if primal:
            sig = 0.5 * jnp.tanh(0.5 * g) + 0.5
            act = g * sig
            hid[:, at] = (act * u).astype(BF16)
            cb[0, :, at] = ((sig + act - act * sig) * u).astype(BF16)
            cb[1, :, at] = act.astype(BF16)
        else:
            hid[:, at] = (
                coef_in[0, :, at].astype(F32) * g + coef_in[1, :, at].astype(F32) * u
            ).astype(BF16)

    before = None
    for f in range(steps):
        for load in up_loads(f):
            load.wait()
        if f + 2 < steps:
            for load in up_loads(f + 2):
                load.start()
        else:
            down_load(f + 2 - steps).start()
        both = dot(xs[...], wb[f, :, : 2 * TILES[f]])
        if f > 0:
            finish(f - 1, before)
        before = both
    finish(steps - 1, before)
    outs = []
    if primal:
        outs.append(pltpu.make_async_copy(cb, coef, csem))
        outs[-1].start()
    for j in range(cols):
        at = slice(j * COLS, (j + 1) * COLS)
        down_load(j).wait()
        out = dot(hid[...], db[j]).astype(BF16)
        for quad in range(2):
            part = dot(ct[quad], out[quad * 4 * SLOTS : (quad + 1) * 4 * SLOTS]).astype(BF16)
            for member in range(4):
                k = quad * 4 + member
                ob[k % 2, k // 2, :, at] = part[member * tokens : (member + 1) * tokens]
        for n, ref in ((1, other), (0, own)):
            outs.append(
                pltpu.make_async_copy(ob.at[n, :, :, at], ref.at[:, :, at], osem.at[n, j])
            )
            outs[-1].start()
    for out in outs:
        out.wait()


def expert(primal, me, messages, weights, more):
    gate, up, down = weights
    width, ff = gate.shape
    tokens = more[1].shape[2] if more else messages[0].shape[0] - INFO
    rows = messages[0].shape[0]
    slots = 8 * SLOTS
    vmem = pl.BlockSpec(memory_space=pltpu.VMEM)
    anywhere = pl.BlockSpec(memory_space=pl.ANY)
    out_shape = [jax.ShapeDtypeStruct((4, tokens, width), BF16)] * 2
    out_specs = [anywhere] * 2
    scratch = [
        pltpu.VMEM((8, rows, width), BF16),
        pltpu.VMEM((len(TILES), width, 2 * TILES[0]), BF16),
        pltpu.VMEM((width // COLS, ff, COLS), BF16),
        pltpu.VMEM((slots, width), BF16),
        pltpu.VMEM((slots, ff), BF16),
        pltpu.VMEM((2, 4 * tokens, 4 * SLOTS), BF16),
        pltpu.VMEM((2, 4, tokens, width), BF16),
        pltpu.SemaphoreType.DMA((8,)),
        pltpu.SemaphoreType.DMA((2, len(TILES))),
        pltpu.SemaphoreType.DMA((width // COLS,)),
        pltpu.SemaphoreType.DMA((2, width // COLS)),
    ]
    if primal:
        out_shape += [
            jax.ShapeDtypeStruct((2, slots, ff), BF16),
            jax.ShapeDtypeStruct((8, SLOTS, tokens), BF16),
            jax.ShapeDtypeStruct((8, SLOTS, tokens), BF16),
        ]
        out_specs += [anywhere, vmem, vmem]
        scratch += [pltpu.VMEM((2, slots, ff), BF16), pltpu.SemaphoreType.DMA]
    return pl.pallas_call(
        functools.partial(expert_kernel, primal, rows),
        out_shape=tuple(out_shape),
        in_specs=[pl.BlockSpec(memory_space=pltpu.SMEM)]
        + [anywhere] * 11
        + [vmem] * len(more),
        out_specs=tuple(out_specs),
        scratch_shapes=scratch,
        compiler_params=pltpu.CompilerParams(vmem_limit_bytes=46 * MIB),
        cost_estimate=pl.CostEstimate(
            flops=6 * slots * width * ff,
            bytes_accessed=6 * width * ff + 24 * tokens * width,
            transcendentals=slots * ff,
        ),
        name="expert_primal" if primal else "expert_tangent",
    )(me, *messages, gate, up, down, *more)


def step_y(x, distance):
    chips = lax.axis_size("exp") // 2
    pairs = [
        (2 * y + c, 2 * ((y + distance) % chips) + c) for y in range(chips) for c in range(2)
    ]
    return lax.ppermute(x, "exp", pairs)


def swap(x):
    count = lax.axis_size("exp")
    return lax.ppermute(x, "exp", [(n, n ^ 1) for n in range(count)])


def spread(x):
    return [x] + [step_y(x, n) for n in SHIFTS[1:]]


def with_swapped(near):
    return [m for one in near for m in (one, swap(one))]


def chip_sums(own, other):
    got = swap(other)
    sums = [own[n].astype(F32) + got[n].astype(F32) for n in range(4)]
    return sums[:1] + [one.astype(BF16) for one in sums[1:]]


def reduce_tokens(base, sums):
    here = sums[0]
    for n, distance in enumerate(SHIFTS):
        if n:
            here = here + step_y(sums[n], -distance).astype(F32)
    return (base + here).astype(BF16)


SHIFTS = (0, 1, -1, 2)


FETCH = (
    ((2, 2), (1, 1), (-1, 0), (2, 1), (1, 0), (2, -1), (2, 0), (0, 2)),
    ((0, 0), (-1, -1), (1, 2), (0, -1), (-1, 2), (0, 1), (1, -1), (-1, 1)),
)
SIDE = 4


def fetch_pairs(offsets):
    return [
        (
            (SIDE * x + z) * 8 + m,
            (SIDE * ((x + offsets[m][0]) % SIDE) + (z + offsets[m][1]) % SIDE) * 8 + m,
        )
        for x in range(SIDE)
        for z in range(SIDE)
        for m in range(8)
    ]


def fetched_heads():
    table = np.zeros((16, 8, 16), np.int32)
    for x in range(SIDE):
        for z in range(SIDE):
            for own in range(8):
                y, c = own // 2, own % 2
                members = [2 * ((y - d) % SIDE) + e for e in (c, 1 - c) for d in SHIFTS]
                table[SIDE * x + z, own] = [
                    SIDE * ((x - f[m][0]) % SIDE) + (z - f[m][1]) % SIDE
                    for m in members
                    for f in FETCH
                ]
    return table


def gather_projection(out_proj, sent):
    part = jnp.concatenate(
        [lax.ppermute(out_proj, ("seq", "exp"), fetch_pairs(f)) for f in FETCH], axis=0
    )
    part, sent = lax.optimization_barrier((part, sent))
    half = part.shape[0] // 2
    up, down = step_y(part, 1), step_y(part, -1)
    far = jnp.concatenate([step_y(up[:half], 1), step_y(down[half:], -1)], axis=0)
    near = [part, up, down, far]
    heads = lax.dynamic_slice(
        jnp.asarray(fetched_heads()),
        (lax.axis_index("seq"), lax.axis_index("exp"), 0),
        (1, 1, 16),
    ).reshape(16)
    return heads, near + [swap(w) for w in near], sent


def shards(
    stream,
    stream_tangent,
    query_rows,
    key_rows,
    value_rows,
    query_tangent,
    key_tangent,
    value_tangent,
    out_proj,
    norm_gain,
    gate_weight,
    up_weight,
    down_weight,
    route_ids,
    route_weights,
):
    tok_dev = stream.shape[1]
    own = lax.axis_index("exp")

    sent = pack(
        [
            query_rows[0],
            key_rows[0],
            value_rows[0],
            query_tangent[0],
            key_tangent[0],
            value_tangent[0],
        ]
    )
    heads, weights, sent = gather_projection(out_proj, sent)
    received = lax.all_to_all(sent, "seq", split_axis=0, concat_axis=0, tiled=True)
    attended = attend(received)
    back = lax.all_to_all(attended, "seq", split_axis=0, concat_axis=0, tiled=True)

    experts_total = lax.axis_size("exp")
    flat_ids = route_ids.reshape(-1)
    onehot = (flat_ids[:, None] == jnp.arange(experts_total, dtype=jnp.int32)[None, :]).astype(
        jnp.int32
    )
    rank_in = jnp.sum((jnp.cumsum(onehot, axis=0) - onehot) * onehot, axis=1)
    rank_in = rank_in.reshape(tok_dev, -1)
    ids = route_ids[0]
    fields = []
    for n in range(2):
        fields += [ids[:, n].astype(BF16), rank_in[:, n].astype(BF16), route_weights[0, :, n]]
    info = jnp.concatenate(
        [jnp.stack(fields), jnp.zeros((INFO - len(fields), tok_dev), BF16)], axis=0
    )

    hidden, hidden_tangent, message, message_tangent = project(
        heads, back, weights, stream[0], stream_tangent[0], norm_gain.reshape(1, -1), info
    )

    me = own.astype(jnp.int32).reshape(1)
    mats = (gate_weight[0], up_weight[0], down_weight[0])
    near, near_tangent = spread(message), spread(message_tangent)
    part, part_other, *more = expert(True, me, with_swapped(near), mats, [])
    part_other, near_tangent = lax.optimization_barrier((part_other, near_tangent))
    tokens_tangent = with_swapped(near_tangent)
    sums = chip_sums(part, part_other)
    tokens_tangent, sums = lax.optimization_barrier((tokens_tangent, sums))
    layer_out = reduce_tokens(hidden, sums)
    dpart, dpart_other = expert(False, me, tokens_tangent, mats, more)
    dpart_other, layer_out = lax.optimization_barrier((dpart_other, layer_out))
    layer_tangent = reduce_tokens(hidden_tangent, chip_sums(dpart, dpart_other))
    return (layer_out[None], layer_tangent[None])


def solution(mesh):
    rows = P("exp", "seq", None)
    in_specs = (rows,) * 8 + (
        P("seq", None),
        P(),
        P("exp", None, None),
        P("exp", None, None),
        P("exp", None, None),
        rows,
        rows,
    )
    return jax.shard_map(
        shards, mesh=mesh, in_specs=in_specs, out_specs=(rows, rows), check_vma=False
    )
```

```python
import functools
import math

import jax
import jax.numpy as jnp
import numpy as np
from jax import lax
from jax.experimental import pallas as pl
from jax.experimental.pallas import tpu as pltpu
from jax.sharding import PartitionSpec as P

HEAD_DIM = 128
BF16 = jnp.bfloat16
F32 = jnp.float32
MIB = 2**20


def dot(a, b):
    return jnp.dot(a, b, preferred_element_type=F32)


def in_hbm(arrays):
    return [pltpu.with_memory_space_constraint(a, pltpu.HBM) for a in arrays]


def pack_kernel(*refs):
    ins, out = refs[:-1], refs[-1]
    heads = out.shape[0]
    for h in range(heads):
        for a, ref in enumerate(ins):
            out[h, a] = ref[:, h * HEAD_DIM : (h + 1) * HEAD_DIM]


def pack(arrays):
    rows, width = arrays[0].shape
    heads = width // HEAD_DIM
    step = 4
    return pl.pallas_call(
        pack_kernel,
        grid=(heads // step,),
        out_shape=jax.ShapeDtypeStruct((heads, len(arrays), rows, HEAD_DIM), BF16),
        in_specs=[pl.BlockSpec((rows, step * HEAD_DIM), lambda i: (0, i))] * len(arrays),
        out_specs=pl.BlockSpec((step, len(arrays), rows, HEAD_DIM), lambda i: (i, 0, 0, 0)),
        cost_estimate=pl.CostEstimate(
            flops=0, bytes_accessed=4 * len(arrays) * rows * width, transcendentals=0
        ),
        name="pack_heads",
    )(*arrays)


KEYS = 512


def attend_kernel(blocks, r_ref, o_ref, t_ref, kt, vv):
    sources, _, rows, _ = r_ref.shape
    i = pl.program_id(0)

    @pl.when(i == 0)
    def _():
        for s in range(sources):
            at = slice(s * rows, (s + 1) * rows)
            kt[:HEAD_DIM, at] = r_ref[s, 1].T
            kt[HEAD_DIM:, at] = r_ref[s, 4].T
            vv[at, :HEAD_DIM] = r_ref[s, 2]
            vv[at, HEAD_DIM:] = r_ref[s, 5]

    scale = 1.0 / math.sqrt(HEAD_DIM)
    q = r_ref[pl.ds(i * blocks, blocks), 0].reshape(blocks * rows, HEAD_DIM)
    dq = r_ref[pl.ds(i * blocks, blocks), 3].reshape(blocks * rows, HEAD_DIM)
    s = dot(q, kt[:HEAD_DIM])
    dqq = jnp.concatenate([dq, q], axis=1)
    factor = scale * math.log2(math.e)
    peak = jnp.max(s, axis=-1, keepdims=True) * factor
    total = row_sum = both = wv = 0.0
    for c in range(0, s.shape[1], KEYS):
        at = slice(c, c + KEYS)
        e = jnp.exp2(s[:, at] * factor - peak)
        total = total + jnp.sum(e, axis=-1, keepdims=True)
        w = e * dot(dqq, kt[:, at])
        row_sum = row_sum + jnp.sum(w, axis=-1, keepdims=True)
        both = both + dot(e.astype(BF16), vv[at])
        wv = wv + dot(w.astype(BF16), vv[at, :HEAD_DIM])
    inv = 1.0 / total
    att = both[:, :HEAD_DIM] * inv
    tan = (wv * scale + both[:, HEAD_DIM:]) * inv - (row_sum * (inv * scale)) * att
    o_ref[...] = att.astype(BF16).reshape(blocks, rows, HEAD_DIM)
    t_ref[...] = tan.astype(BF16).reshape(blocks, rows, HEAD_DIM)


def attend(received, blocks=4):
    sources, _, rows, _ = received.shape
    seq_len = sources * rows
    return pl.pallas_call(
        functools.partial(attend_kernel, blocks),
        grid=(sources // blocks,),
        out_shape=(pltpu.HBM((sources, rows, HEAD_DIM), BF16),) * 2,
        in_specs=[pl.BlockSpec(received.shape, lambda i: (0, 0, 0, 0))],
        out_specs=(pl.BlockSpec((blocks, rows, HEAD_DIM), lambda i: (i, 0, 0)),) * 2,
        scratch_shapes=[
            pltpu.VMEM((2 * HEAD_DIM, seq_len), BF16),
            pltpu.VMEM((seq_len, 2 * HEAD_DIM), BF16),
        ],
        compiler_params=pltpu.CompilerParams(vmem_limit_bytes=32 * MIB),
        cost_estimate=pl.CostEstimate(
            flops=16 * seq_len * seq_len * HEAD_DIM,
            bytes_accessed=16 * seq_len * HEAD_DIM,
            transcendentals=seq_len * seq_len,
        ),
        name="attend_head",
    )(received)


def project_kernel(primal, heads, *refs):
    w_refs, refs = refs[:16], refs[16:]
    back, s_in, g_ref, more, h_ref, m_ref, x, wv, sem, a_ref, s_ref, asem = refs
    rows, width = h_ref.shape
    loads = [
        pltpu.make_async_copy(ref, wv.at[n * HEAD_DIM : (n + 1) * HEAD_DIM], sem.at[n])
        for n, ref in enumerate(w_refs)
    ]
    firsts = [
        pltpu.make_async_copy(a, b, asem.at[n])
        for n, (a, b) in enumerate(((back, a_ref), (s_in, s_ref)))
    ]
    for load in firsts + loads:
        load.start()
    for load in firsts:
        load.wait()
    for h in range(a_ref.shape[0]):
        x[:, h * HEAD_DIM : (h + 1) * HEAD_DIM] = a_ref[heads[h]]
    half, tile = width // 2, 512
    for part in range(2):
        for load in loads[8 * part : 8 * part + 8]:
            load.wait()
        k = slice(part * half, (part + 1) * half)
        for n in range(0, width, tile):
            at = slice(n, n + tile)
            before = s_ref[:, at].astype(F32) if part == 0 else h_ref[:, at]
            h_ref[:, at] = before + dot(x[:, k], wv[k, at])
    gain = g_ref[...].astype(F32)
    if primal:
        hid = h_ref[...]
        inverse = lax.rsqrt(jnp.mean(hid * hid, axis=-1, keepdims=True) + 1e-06)
        normed = (hid * inverse * gain).astype(BF16)
        middle, info = rows // 2, more.shape[0]
        m_ref[:middle] = normed[:middle]
        m_ref[middle : middle + info] = jnp.zeros((info, width), BF16)
        m_ref[middle : middle + info, : more.shape[1]] = more[...]
        m_ref[middle + info :] = normed[middle:]
    else:
        hid, tan = more[...], h_ref[...]
        inverse = lax.rsqrt(jnp.mean(hid * hid, axis=-1, keepdims=True) + 1e-06)
        cross = jnp.mean(hid * tan, axis=-1, keepdims=True)
        m_ref[...] = (
            gain * (tan * inverse - hid * (inverse * inverse * inverse) * cross)
        ).astype(BF16)


def project(primal, heads, attended, weights, stream, gain, more):
    rows, width = stream.shape
    vmem = pl.BlockSpec(memory_space=pltpu.VMEM)
    hbm = pl.BlockSpec(memory_space=pltpu.HBM)
    sent = rows + more.shape[0] if primal else rows
    return pl.pallas_call(
        functools.partial(project_kernel, primal),
        out_shape=(
            jax.ShapeDtypeStruct((rows, width), F32),
            jax.ShapeDtypeStruct((sent, width), BF16),
        ),
        in_specs=[pl.BlockSpec(memory_space=pltpu.SMEM)]
        + [pl.BlockSpec(memory_space=pl.ANY)] * 17
        + [hbm]
        + [vmem] * 2,
        out_specs=(vmem,) * 2,
        scratch_shapes=[
            pltpu.VMEM((rows, width), BF16),
            pltpu.VMEM((width, width), BF16),
            pltpu.SemaphoreType.DMA((16,)),
            pltpu.VMEM(attended.shape, BF16),
            pltpu.VMEM((rows, width), BF16),
            pltpu.SemaphoreType.DMA((2,)),
        ],
        compiler_params=pltpu.CompilerParams(vmem_limit_bytes=32 * MIB),
        cost_estimate=pl.CostEstimate(
            flops=2 * rows * width * width, bytes_accessed=3 * width * width, transcendentals=0
        ),
        name="project_primal" if primal else "project_tangent",
    )(heads, *in_hbm([*weights, attended, stream]), gain, more)


SLOTS = 64
INFO = 16
TILES = (512, 512, 384)
COLS = 1024


def expert_kernel(primal, rows, *refs):
    it = iter(refs)
    take = lambda n: [next(it) for _ in range(n)]
    (me,) = take(1)
    messages = take(8)
    gate, up, down = take(3)
    if primal:
        own, other, coef, disp, comb = take(5)
    else:
        coef_in, disp, comb = take(3)
        own, other = take(2)
    mb, wb, db, xs, hid, ct, ob, msem, wsem, dsem, osem = take(11)
    if primal:
        cb, csem = take(2)
    tokens, width = own.shape[1:]
    steps, cols = len(TILES), width // COLS
    starts = [sum(TILES[:n]) for n in range(steps)]
    loads = [pltpu.make_async_copy(a, b, msem.at[n]) for n, (a, b) in enumerate(zip(messages, [mb.at[k] for k in range(8)]))]
    for load in loads:
        load.start()

    def up_loads(f):
        at, tile = slice(starts[f], starts[f] + TILES[f]), TILES[f]
        return (
            pltpu.make_async_copy(gate.at[:, at], wb.at[f, :, :tile], wsem.at[0, f]),
            pltpu.make_async_copy(up.at[:, at], wb.at[f, :, tile : 2 * tile], wsem.at[1, f]),
        )

    def down_load(j):
        at = slice(j * COLS, (j + 1) * COLS)
        return pltpu.make_async_copy(down.at[:, at], db.at[j], dsem.at[j])

    for load in up_loads(0):
        load.start()
    ct[...] = jnp.zeros(ct.shape, BF16)
    for load in loads:
        load.wait()
    for load in up_loads(1):
        load.start()

    half = tokens // 2
    none = jnp.zeros((SLOTS, tokens), F32)

    def diagonal(first, second):
        return jnp.concatenate(
            [
                jnp.concatenate([first, none], axis=1),
                jnp.concatenate([none, second], axis=1),
            ],
            axis=0,
        )

    def slots_of(k):
        if not primal:
            return disp[k].astype(F32), comb[k].astype(F32), mb[k]
        info = mb[k, half : half + INFO, :tokens].astype(F32)
        slot = lax.broadcasted_iota(jnp.int32, (SLOTS, tokens), 0).astype(F32)
        mine = me[0].astype(F32)
        d, c = none, none
        for n in range(2):
            hit = (info[3 * n : 3 * n + 1] == mine) & (info[3 * n + 1 : 3 * n + 2] == slot)
            d = d + jnp.where(hit, 1.0, 0.0)
            c = c + jnp.where(hit, info[3 * n + 2 : 3 * n + 3], 0.0)
        disp[k] = d.astype(BF16)
        comb[k] = c.astype(BF16)
        return d, c, jnp.concatenate([mb[k, :half], mb[k, half + INFO :]], axis=0)

    def pair_step(p, carry):
        d0, c0, tok0 = slots_of(2 * p)
        d1, c1, tok1 = slots_of(2 * p + 1)
        q = p % 2
        rows_at = pl.ds(pl.multiple_of(q * 2 * tokens, 2 * tokens), 2 * tokens)
        cols_at = pl.ds(pl.multiple_of(q * 2 * SLOTS, 2 * SLOTS), 2 * SLOTS)
        ct[p // 2, rows_at, cols_at] = diagonal(c0, c1).T.astype(BF16)
        at = pl.ds(pl.multiple_of(p * 2 * SLOTS, 2 * SLOTS), 2 * SLOTS)
        xs[at] = dot(
            diagonal(d0, d1).astype(BF16), jnp.concatenate([tok0, tok1], axis=0)
        ).astype(BF16)
        return carry

    lax.fori_loop(0, 4, pair_step, 0)

    def finish(f, both):
        tile = TILES[f]
        at = slice(starts[f], starts[f] + tile)
        g, u = both[:, :tile], both[:, tile:]
        if primal:
            sig = 0.5 * jnp.tanh(0.5 * g) + 0.5
            act = g * sig
            hid[:, at] = (act * u).astype(BF16)
            cb[0, :, at] = ((sig + act - act * sig) * u).astype(BF16)
            cb[1, :, at] = act.astype(BF16)
        else:
            hid[:, at] = (
                coef_in[0, :, at].astype(F32) * g + coef_in[1, :, at].astype(F32) * u
            ).astype(BF16)

    before = None
    for f in range(steps):
        for load in up_loads(f):
            load.wait()
        if f + 2 < steps:
            for load in up_loads(f + 2):
                load.start()
        else:
            down_load(f + 2 - steps).start()
        both = dot(xs[...], wb[f, :, : 2 * TILES[f]])
        if f > 0:
            finish(f - 1, before)
        before = both
    finish(steps - 1, before)
    outs = []
    if primal:
        outs.append(pltpu.make_async_copy(cb, coef, csem))
        outs[-1].start()
    for j in range(cols):
        at = slice(j * COLS, (j + 1) * COLS)
        down_load(j).wait()
        out = dot(hid[...], db[j]).astype(BF16)
        for quad in range(2):
            part = dot(ct[quad], out[quad * 4 * SLOTS : (quad + 1) * 4 * SLOTS]).astype(BF16)
            for member in range(4):
                k = quad * 4 + member
                ob[k % 2, k // 2, :, at] = part[member * tokens : (member + 1) * tokens]
        for n, ref in ((1, other), (0, own)):
            outs.append(
                pltpu.make_async_copy(ob.at[n, :, :, at], ref.at[:, :, at], osem.at[n, j])
            )
            outs[-1].start()
    for out in outs:
        out.wait()


def expert(primal, me, messages, weights, more):
    gate, up, down = weights
    width, ff = gate.shape
    tokens = more[1].shape[2] if more else messages[0].shape[0] - INFO
    rows = messages[0].shape[0]
    slots = 8 * SLOTS
    vmem = pl.BlockSpec(memory_space=pltpu.VMEM)
    anywhere = pl.BlockSpec(memory_space=pl.ANY)
    out_shape = [jax.ShapeDtypeStruct((4, tokens, width), BF16)] * 2
    out_specs = [anywhere] * 2
    scratch = [
        pltpu.VMEM((8, rows, width), BF16),
        pltpu.VMEM((len(TILES), width, 2 * TILES[0]), BF16),
        pltpu.VMEM((width // COLS, ff, COLS), BF16),
        pltpu.VMEM((slots, width), BF16),
        pltpu.VMEM((slots, ff), BF16),
        pltpu.VMEM((2, 4 * tokens, 4 * SLOTS), BF16),
        pltpu.VMEM((2, 4, tokens, width), BF16),
        pltpu.SemaphoreType.DMA((8,)),
        pltpu.SemaphoreType.DMA((2, len(TILES))),
        pltpu.SemaphoreType.DMA((width // COLS,)),
        pltpu.SemaphoreType.DMA((2, width // COLS)),
    ]
    if primal:
        out_shape += [
            jax.ShapeDtypeStruct((2, slots, ff), BF16),
            jax.ShapeDtypeStruct((8, SLOTS, tokens), BF16),
            jax.ShapeDtypeStruct((8, SLOTS, tokens), BF16),
        ]
        out_specs += [anywhere, vmem, vmem]
        scratch += [pltpu.VMEM((2, slots, ff), BF16), pltpu.SemaphoreType.DMA]
    return pl.pallas_call(
        functools.partial(expert_kernel, primal, rows),
        out_shape=tuple(out_shape),
        in_specs=[pl.BlockSpec(memory_space=pltpu.SMEM)]
        + [anywhere] * 11
        + [vmem] * len(more),
        out_specs=tuple(out_specs),
        scratch_shapes=scratch,
        compiler_params=pltpu.CompilerParams(vmem_limit_bytes=46 * MIB),
        cost_estimate=pl.CostEstimate(
            flops=0 if primal else 6 * slots * width * ff,
            bytes_accessed=0 if primal else 6 * width * ff + 24 * tokens * width,
            transcendentals=0 if primal else slots * ff,
        ),
        name="expert_primal" if primal else "expert_tangent",
    )(me, *in_hbm([*messages, gate, up, down]), *more)


def step_y(x, distance):
    chips = lax.axis_size("exp") // 2
    pairs = [
        (2 * y + c, 2 * ((y + distance) % chips) + c) for y in range(chips) for c in range(2)
    ]
    return lax.ppermute(x, "exp", pairs)


def swap(x):
    count = lax.axis_size("exp")
    return lax.ppermute(x, "exp", [(n, n ^ 1) for n in range(count)])


def spread(x):
    return [x] + [step_y(x, n) for n in SHIFTS[1:]]


def with_swapped(near):
    return [m for one in near for m in (one, swap(one))]


def chip_sums(own, other):
    got = swap(other)
    sums = [own[n].astype(F32) + got[n].astype(F32) for n in range(4)]
    return sums[:1] + [one.astype(BF16) for one in sums[1:]]


def reduce_tokens(base, sums):
    here = sums[0]
    for n, distance in enumerate(SHIFTS):
        if n:
            here = here + step_y(sums[n], -distance).astype(F32)
    return (base + here).astype(BF16)


SHIFTS = (0, 1, -1, 2)


FETCH = (
    ((2, 2), (1, 1), (-1, 0), (2, 1), (1, 0), (2, -1), (2, 0), (0, 2)),
    ((0, 0), (-1, -1), (1, 2), (0, -1), (-1, 2), (0, 1), (1, -1), (-1, 1)),
)
SIDE = 4


def fetch_pairs(offsets):
    return [
        (
            (SIDE * x + z) * 8 + m,
            (SIDE * ((x + offsets[m][0]) % SIDE) + (z + offsets[m][1]) % SIDE) * 8 + m,
        )
        for x in range(SIDE)
        for z in range(SIDE)
        for m in range(8)
    ]


def fetched_heads():
    table = np.zeros((16, 8, 16), np.int32)
    for x in range(SIDE):
        for z in range(SIDE):
            for own in range(8):
                y, c = own // 2, own % 2
                members = [2 * ((y - d) % SIDE) + e for e in (c, 1 - c) for d in SHIFTS]
                table[SIDE * x + z, own] = [
                    SIDE * ((x - f[m][0]) % SIDE) + (z - f[m][1]) % SIDE
                    for m in members
                    for f in FETCH
                ]
    return table


def gather_projection(out_proj, sent):
    first, second = [lax.ppermute(out_proj, ("seq", "exp"), fetch_pairs(f)) for f in FETCH]
    first, second, sent = lax.optimization_barrier((first, second, sent))
    up, down = [step_y(w, 1) for w in (first, second)], [step_y(w, -1) for w in (first, second)]
    near = [first, second] + up + down + [step_y(up[0], 1), step_y(down[1], -1)]
    heads = lax.dynamic_slice(
        jnp.asarray(fetched_heads()),
        (lax.axis_index("seq"), lax.axis_index("exp"), 0),
        (1, 1, 16),
    ).reshape(16)
    return heads, near + [swap(w) for w in near], sent


def shards(
    stream,
    stream_tangent,
    query_rows,
    key_rows,
    value_rows,
    query_tangent,
    key_tangent,
    value_tangent,
    out_proj,
    norm_gain,
    gate_weight,
    up_weight,
    down_weight,
    route_ids,
    route_weights,
):
    tok_dev = stream.shape[1]
    own = lax.axis_index("exp")

    sent = pack(
        [
            query_rows[0],
            key_rows[0],
            value_rows[0],
            query_tangent[0],
            key_tangent[0],
            value_tangent[0],
        ]
    )
    heads, weights, sent = gather_projection(out_proj, sent)
    received = lax.all_to_all(sent, "seq", split_axis=0, concat_axis=0, tiled=True)
    attended, attended_tangent = attend(received)
    back = lax.all_to_all(attended, "seq", split_axis=0, concat_axis=0, tiled=True)

    experts_total = lax.axis_size("exp")
    flat_ids = route_ids.reshape(-1)
    onehot = (flat_ids[:, None] == jnp.arange(experts_total, dtype=jnp.int32)[None, :]).astype(
        jnp.int32
    )
    rank_in = jnp.sum((jnp.cumsum(onehot, axis=0) - onehot) * onehot, axis=1)
    rank_in = rank_in.reshape(tok_dev, -1)
    ids = route_ids[0]
    fields = []
    for n in range(2):
        fields += [ids[:, n].astype(BF16), rank_in[:, n].astype(BF16), route_weights[0, :, n]]
    info = jnp.concatenate(
        [jnp.stack(fields), jnp.zeros((INFO - len(fields), tok_dev), BF16)], axis=0
    )

    gain = norm_gain.reshape(1, -1)
    hidden, message = project(True, heads, back, weights, stream[0], gain, info)
    attended_tangent, message = lax.optimization_barrier((attended_tangent, message))
    back = lax.all_to_all(attended_tangent, "seq", split_axis=0, concat_axis=0, tiled=True)
    hidden_tangent, message_tangent = project(
        False, heads, back, weights, stream_tangent[0], gain, hidden
    )

    me = own.astype(jnp.int32).reshape(1)
    mats = (gate_weight[0], up_weight[0], down_weight[0])
    near, near_tangent = spread(message), spread(message_tangent)
    part, part_other, *more = expert(True, me, with_swapped(near), mats, [])
    part_other, near_tangent = lax.optimization_barrier((part_other, near_tangent))
    tokens_tangent = with_swapped(near_tangent)
    sums = chip_sums(part, part_other)
    tokens_tangent, sums = lax.optimization_barrier((tokens_tangent, sums))
    layer_out = reduce_tokens(hidden, sums)
    dpart, dpart_other = expert(False, me, tokens_tangent, mats, more)
    dpart_other, layer_out = lax.optimization_barrier((dpart_other, layer_out))
    layer_tangent = reduce_tokens(hidden_tangent, chip_sums(dpart, dpart_other))
    return (layer_out[None], layer_tangent[None])


def solution(mesh):
    rows = P("exp", "seq", None)
    in_specs = (rows,) * 8 + (
        P("seq", None),
        P(),
        P("exp", None, None),
        P("exp", None, None),
        P("exp", None, None),
        rows,
        rows,
    )
    return jax.shard_map(
        shards, mesh=mesh, in_specs=in_specs, out_specs=(rows, rows), check_vma=False
    )
```

```python
import functools
import math

import jax
import jax.numpy as jnp
import numpy as np
from jax import lax
from jax.experimental import pallas as pl
from jax.experimental.pallas import tpu as pltpu
from jax.sharding import PartitionSpec as P

HEAD_DIM = 128
BF16 = jnp.bfloat16
F32 = jnp.float32
MIB = 2**20


def dot(a, b):
    return jnp.dot(a, b, preferred_element_type=F32)


def in_hbm(arrays):
    return [pltpu.with_memory_space_constraint(a, pltpu.HBM) for a in arrays]


def pack_kernel(*refs):
    ins, out = refs[:-1], refs[-1]
    heads = out.shape[0]
    for h in range(heads):
        for a, ref in enumerate(ins):
            out[h, a] = ref[:, h * HEAD_DIM : (h + 1) * HEAD_DIM]


def pack(arrays):
    rows, width = arrays[0].shape
    heads = width // HEAD_DIM
    step = 4
    return pl.pallas_call(
        pack_kernel,
        grid=(heads // step,),
        out_shape=jax.ShapeDtypeStruct((heads, len(arrays), rows, HEAD_DIM), BF16),
        in_specs=[pl.BlockSpec((rows, step * HEAD_DIM), lambda i: (0, i))] * len(arrays),
        out_specs=pl.BlockSpec((step, len(arrays), rows, HEAD_DIM), lambda i: (i, 0, 0, 0)),
        cost_estimate=pl.CostEstimate(
            flops=0, bytes_accessed=4 * len(arrays) * rows * width, transcendentals=0
        ),
        name="pack_heads",
    )(*arrays)


KEYS = 512


def attend_kernel(blocks, r_ref, o_ref, t_ref, kt, vv):
    sources, _, rows, _ = r_ref.shape
    i = pl.program_id(0)

    @pl.when(i == 0)
    def _():
        for s in range(sources):
            at = slice(s * rows, (s + 1) * rows)
            kt[:HEAD_DIM, at] = r_ref[s, 1].T
            kt[HEAD_DIM:, at] = r_ref[s, 4].T
            vv[at, :HEAD_DIM] = r_ref[s, 2]
            vv[at, HEAD_DIM:] = r_ref[s, 5]

    scale = 1.0 / math.sqrt(HEAD_DIM)
    q = r_ref[pl.ds(i * blocks, blocks), 0].reshape(blocks * rows, HEAD_DIM)
    dq = r_ref[pl.ds(i * blocks, blocks), 3].reshape(blocks * rows, HEAD_DIM)
    s = dot(q, kt[:HEAD_DIM])
    dqq = jnp.concatenate([dq, q], axis=1)
    factor = scale * math.log2(math.e)
    peak = jnp.max(s, axis=-1, keepdims=True) * factor
    total = row_sum = both = wv = 0.0
    for c in range(0, s.shape[1], KEYS):
        at = slice(c, c + KEYS)
        e = jnp.exp2(s[:, at] * factor - peak)
        total = total + jnp.sum(e, axis=-1, keepdims=True)
        w = e * dot(dqq, kt[:, at])
        row_sum = row_sum + jnp.sum(w, axis=-1, keepdims=True)
        both = both + dot(e.astype(BF16), vv[at])
        wv = wv + dot(w.astype(BF16), vv[at, :HEAD_DIM])
    inv = 1.0 / total
    att = both[:, :HEAD_DIM] * inv
    tan = (wv * scale + both[:, HEAD_DIM:]) * inv - (row_sum * (inv * scale)) * att
    o_ref[...] = att.astype(BF16).reshape(blocks, rows, HEAD_DIM)
    t_ref[...] = tan.astype(BF16).reshape(blocks, rows, HEAD_DIM)


def attend(received, blocks=4):
    sources, _, rows, _ = received.shape
    seq_len = sources * rows
    return pl.pallas_call(
        functools.partial(attend_kernel, blocks),
        grid=(sources // blocks,),
        out_shape=(pltpu.HBM((sources, rows, HEAD_DIM), BF16),) * 2,
        in_specs=[pl.BlockSpec(received.shape, lambda i: (0, 0, 0, 0))],
        out_specs=(pl.BlockSpec((blocks, rows, HEAD_DIM), lambda i: (i, 0, 0)),) * 2,
        scratch_shapes=[
            pltpu.VMEM((2 * HEAD_DIM, seq_len), BF16),
            pltpu.VMEM((seq_len, 2 * HEAD_DIM), BF16),
        ],
        compiler_params=pltpu.CompilerParams(vmem_limit_bytes=32 * MIB),
        cost_estimate=pl.CostEstimate(
            flops=16 * seq_len * seq_len * HEAD_DIM,
            bytes_accessed=16 * seq_len * HEAD_DIM,
            transcendentals=seq_len * seq_len,
        ),
        name="attend_head",
    )(received)


def project_kernel(primal, heads, *refs):
    w_refs, refs = refs[:16], refs[16:]
    s_in, a_ref, g_ref, more, h_ref, m_ref, x, wv, sem, s_ref, asem = refs
    rows, width = h_ref.shape
    loads = [
        pltpu.make_async_copy(ref, wv.at[n * HEAD_DIM : (n + 1) * HEAD_DIM], sem.at[n])
        for n, ref in enumerate(w_refs)
    ]
    stream_load = pltpu.make_async_copy(s_in, s_ref, asem)
    for load in loads + [stream_load]:
        load.start()
    for h in range(a_ref.shape[0]):
        x[:, h * HEAD_DIM : (h + 1) * HEAD_DIM] = a_ref[heads[h]]
    half, tile = width // 2, 512
    stream_load.wait()
    for part in range(2):
        for load in loads[8 * part : 8 * part + 8]:
            load.wait()
        k = slice(part * half, (part + 1) * half)
        for n in range(0, width, tile):
            at = slice(n, n + tile)
            before = s_ref[:, at].astype(F32) if part == 0 else h_ref[:, at]
            h_ref[:, at] = before + dot(x[:, k], wv[k, at])
    gain = g_ref[...].astype(F32)
    if primal:
        hid = h_ref[...]
        inverse = lax.rsqrt(jnp.mean(hid * hid, axis=-1, keepdims=True) + 1e-06)
        normed = (hid * inverse * gain).astype(BF16)
        middle, info = rows // 2, more.shape[0]
        m_ref[:middle] = normed[:middle]
        m_ref[middle : middle + info] = jnp.zeros((info, width), BF16)
        m_ref[middle : middle + info, : more.shape[1]] = more[...]
        m_ref[middle + info :] = normed[middle:]
    else:
        hid, tan = more[...], h_ref[...]
        inverse = lax.rsqrt(jnp.mean(hid * hid, axis=-1, keepdims=True) + 1e-06)
        cross = jnp.mean(hid * tan, axis=-1, keepdims=True)
        m_ref[...] = (
            gain * (tan * inverse - hid * (inverse * inverse * inverse) * cross)
        ).astype(BF16)


def project(primal, heads, attended, weights, stream, gain, more):
    rows, width = stream.shape
    vmem = pl.BlockSpec(memory_space=pltpu.VMEM)
    hbm = pl.BlockSpec(memory_space=pltpu.HBM)
    sent = rows + more.shape[0] if primal else rows
    return pl.pallas_call(
        functools.partial(project_kernel, primal),
        out_shape=(
            jax.ShapeDtypeStruct((rows, width), F32),
            jax.ShapeDtypeStruct((sent, width), BF16),
        ),
        in_specs=[pl.BlockSpec(memory_space=pltpu.SMEM)]
        + [hbm] * 17
        + [vmem] * 3,
        out_specs=(vmem,) * 2,
        scratch_shapes=[
            pltpu.VMEM((rows, width), BF16),
            pltpu.VMEM((width, width), BF16),
            pltpu.SemaphoreType.DMA((16,)),
            pltpu.VMEM((rows, width), BF16),
            pltpu.SemaphoreType.DMA,
        ],
        compiler_params=pltpu.CompilerParams(vmem_limit_bytes=32 * MIB),
        cost_estimate=pl.CostEstimate(
            flops=2 * rows * width * width, bytes_accessed=3 * width * width, transcendentals=0
        ),
        name="project_primal" if primal else "project_tangent",
    )(heads, *in_hbm([*weights, stream]), attended, gain, more)


SLOTS = 64
INFO = 16
TILES = (512, 512, 384)
COLS = 1024


def expert_kernel(primal, rows, *refs):
    it = iter(refs)
    take = lambda n: [next(it) for _ in range(n)]
    (me,) = take(1)
    messages = take(8)
    gate, up, down = take(3)
    if primal:
        own, other, coef, disp, comb = take(5)
    else:
        coef, disp, comb = take(3)
        own, other = take(2)
    mb, wb, db, xs, hid, ct, ob, msem, wsem, dsem, osem = take(11)
    cb, csem = take(2)
    tokens, width = own.shape[1:]
    steps, cols = len(TILES), width // COLS
    starts = [sum(TILES[:n]) for n in range(steps)]
    loads = [pltpu.make_async_copy(a, b, msem.at[n]) for n, (a, b) in enumerate(zip(messages, [mb.at[k] for k in range(8)]))]
    for load in loads:
        load.start()

    def up_loads(f):
        at, tile = slice(starts[f], starts[f] + TILES[f]), TILES[f]
        return (
            pltpu.make_async_copy(gate.at[:, at], wb.at[f, :, :tile], wsem.at[0, f]),
            pltpu.make_async_copy(up.at[:, at], wb.at[f, :, tile : 2 * tile], wsem.at[1, f]),
        )

    def down_load(j):
        at = slice(j * COLS, (j + 1) * COLS)
        return pltpu.make_async_copy(down.at[:, at], db.at[j], dsem.at[j])

    for load in up_loads(0):
        load.start()
    ct[...] = jnp.zeros(ct.shape, BF16)
    for load in loads:
        load.wait()
    for load in up_loads(1):
        load.start()

    if not primal:
        coef_load = pltpu.make_async_copy(coef, cb, csem)
        coef_load.start()
    half = tokens // 2
    none = jnp.zeros((SLOTS, tokens), F32)

    def diagonal(first, second):
        return jnp.concatenate(
            [
                jnp.concatenate([first, none], axis=1),
                jnp.concatenate([none, second], axis=1),
            ],
            axis=0,
        )

    def slots_of(k):
        if not primal:
            return disp[k].astype(F32), comb[k].astype(F32), mb[k]
        info = mb[k, half : half + INFO, :tokens].astype(F32)
        slot = lax.broadcasted_iota(jnp.int32, (SLOTS, tokens), 0).astype(F32)
        mine = me[0].astype(F32)
        d, c = none, none
        for n in range(2):
            hit = (info[3 * n : 3 * n + 1] == mine) & (info[3 * n + 1 : 3 * n + 2] == slot)
            d = d + jnp.where(hit, 1.0, 0.0)
            c = c + jnp.where(hit, info[3 * n + 2 : 3 * n + 3], 0.0)
        disp[k] = d.astype(BF16)
        comb[k] = c.astype(BF16)
        return d, c, jnp.concatenate([mb[k, :half], mb[k, half + INFO :]], axis=0)

    def pair_step(p, carry):
        d0, c0, tok0 = slots_of(2 * p)
        d1, c1, tok1 = slots_of(2 * p + 1)
        q = p % 2
        rows_at = pl.ds(pl.multiple_of(q * 2 * tokens, 2 * tokens), 2 * tokens)
        cols_at = pl.ds(pl.multiple_of(q * 2 * SLOTS, 2 * SLOTS), 2 * SLOTS)
        ct[p // 2, rows_at, cols_at] = diagonal(c0, c1).T.astype(BF16)
        at = pl.ds(pl.multiple_of(p * 2 * SLOTS, 2 * SLOTS), 2 * SLOTS)
        xs[at] = dot(
            diagonal(d0, d1).astype(BF16), jnp.concatenate([tok0, tok1], axis=0)
        ).astype(BF16)
        return carry

    lax.fori_loop(0, 4, pair_step, 0)

    def finish(f, both):
        tile = TILES[f]
        at = slice(starts[f], starts[f] + tile)
        g, u = both[:, :tile], both[:, tile:]
        if primal:
            sig = 0.5 * jnp.tanh(0.5 * g) + 0.5
            act = g * sig
            hid[:, at] = (act * u).astype(BF16)
            cb[0, :, at] = ((sig + act - act * sig) * u).astype(BF16)
            cb[1, :, at] = act.astype(BF16)
        else:
            hid[:, at] = (
                cb[0, :, at].astype(F32) * g + cb[1, :, at].astype(F32) * u
            ).astype(BF16)

    before = None
    for f in range(steps):
        for load in up_loads(f):
            load.wait()
        if f + 2 < steps:
            for load in up_loads(f + 2):
                load.start()
        else:
            down_load(f + 2 - steps).start()
        both = dot(xs[...], wb[f, :, : 2 * TILES[f]])
        if f == 1 and not primal:
            coef_load.wait()
        if f > 0:
            finish(f - 1, before)
        before = both
    finish(steps - 1, before)
    outs = []
    if primal:
        outs.append(pltpu.make_async_copy(cb, coef, csem))
        outs[-1].start()
    for j in range(cols):
        at = slice(j * COLS, (j + 1) * COLS)
        down_load(j).wait()
        out = dot(hid[...], db[j]).astype(BF16)
        for quad in range(2):
            part = dot(ct[quad], out[quad * 4 * SLOTS : (quad + 1) * 4 * SLOTS]).astype(BF16)
            for member in range(4):
                k = quad * 4 + member
                ob[k % 2, k // 2, :, at] = part[member * tokens : (member + 1) * tokens]
        for n, ref in ((1, other), (0, own)):
            outs.append(
                pltpu.make_async_copy(ob.at[n, :, :, at], ref.at[:, :, at], osem.at[n, j])
            )
            outs[-1].start()
    for out in outs:
        out.wait()


def expert(primal, me, messages, weights, more):
    gate, up, down = weights
    width, ff = gate.shape
    tokens = more[1].shape[2] if more else messages[0].shape[0] - INFO
    rows = messages[0].shape[0]
    slots = 8 * SLOTS
    vmem = pl.BlockSpec(memory_space=pltpu.VMEM)
    anywhere = pl.BlockSpec(memory_space=pl.ANY)
    out_shape = [jax.ShapeDtypeStruct((4, tokens, width), BF16)] * 2
    out_specs = [anywhere] * 2
    scratch = [
        pltpu.VMEM((8, rows, width), BF16),
        pltpu.VMEM((len(TILES), width, 2 * TILES[0]), BF16),
        pltpu.VMEM((width // COLS, ff, COLS), BF16),
        pltpu.VMEM((slots, width), BF16),
        pltpu.VMEM((slots, ff), BF16),
        pltpu.VMEM((2, 4 * tokens, 4 * SLOTS), BF16),
        pltpu.VMEM((2, 4, tokens, width), BF16),
        pltpu.SemaphoreType.DMA((8,)),
        pltpu.SemaphoreType.DMA((2, len(TILES))),
        pltpu.SemaphoreType.DMA((width // COLS,)),
        pltpu.SemaphoreType.DMA((2, width // COLS)),
        pltpu.VMEM((2, slots, ff), BF16),
        pltpu.SemaphoreType.DMA,
    ]
    if primal:
        out_shape += [
            jax.ShapeDtypeStruct((2, slots, ff), BF16),
            jax.ShapeDtypeStruct((8, SLOTS, tokens), BF16),
            jax.ShapeDtypeStruct((8, SLOTS, tokens), BF16),
        ]
        out_specs += [anywhere, vmem, vmem]
    return pl.pallas_call(
        functools.partial(expert_kernel, primal, rows),
        out_shape=tuple(out_shape),
        in_specs=[pl.BlockSpec(memory_space=pltpu.SMEM)]
        + [anywhere] * 11
        + [anywhere, vmem, vmem][: len(more)],
        out_specs=tuple(out_specs),
        scratch_shapes=scratch,
        compiler_params=pltpu.CompilerParams(vmem_limit_bytes=46 * MIB),
        cost_estimate=pl.CostEstimate(
            flops=0 if primal else 6 * slots * width * ff,
            bytes_accessed=0 if primal else 6 * width * ff + 24 * tokens * width,
            transcendentals=0 if primal else slots * ff,
        ),
        name="expert_primal" if primal else "expert_tangent",
    )(me, *in_hbm([*messages, gate, up, down]), *more)


def step_y(x, distance):
    chips = lax.axis_size("exp") // 2
    pairs = [
        (2 * y + c, 2 * ((y + distance) % chips) + c) for y in range(chips) for c in range(2)
    ]
    return lax.ppermute(x, "exp", pairs)


def swap(x):
    count = lax.axis_size("exp")
    return lax.ppermute(x, "exp", [(n, n ^ 1) for n in range(count)])


def spread(x):
    return [x] + [step_y(x, n) for n in SHIFTS[1:]]


def with_swapped(near):
    return [m for one in near for m in (one, swap(one))]


def chip_sums(own, other):
    got = swap(other)
    sums = [own[n].astype(F32) + got[n].astype(F32) for n in range(4)]
    return sums[:1] + [one.astype(BF16) for one in sums[1:]]


def send_sums(sums):
    return [step_y(one, -n) for one, n in zip(sums[1:], SHIFTS[1:])]


def forward_sums(sums):
    here, before, after, far = sums
    half = far.shape[0] // 2
    via_up, via_down = step_y(far[:half], 1), step_y(far[half:], -1)
    free = [step_y(after[half:], 1), step_y(before[:half], -1)]
    add = lambda a, b: (a.astype(F32) + b.astype(F32)).astype(BF16)
    late = [step_y(add(after[:half], via_up), 1), step_y(add(before[half:], via_down), -1)]
    return [
        jnp.concatenate([late[0], free[0]], axis=0),
        jnp.concatenate([free[1], late[1]], axis=0),
    ]


def finish(base, sums, arrived):
    here = sums[0]
    for one in arrived:
        here = here + one.astype(F32)
    return (base + here).astype(BF16)


SHIFTS = (0, 1, -1, 2)


FETCH = (
    ((2, 2), (1, 1), (-1, 0), (2, 1), (1, 0), (2, -1), (2, 0), (0, 2)),
    ((0, 0), (-1, -1), (1, 2), (0, -1), (-1, 2), (0, 1), (1, -1), (-1, 1)),
)
SIDE = 4


def fetch_pairs(offsets):
    return [
        (
            (SIDE * x + z) * 8 + m,
            (SIDE * ((x + offsets[m][0]) % SIDE) + (z + offsets[m][1]) % SIDE) * 8 + m,
        )
        for x in range(SIDE)
        for z in range(SIDE)
        for m in range(8)
    ]


def fetched_heads():
    table = np.zeros((16, 8, 16), np.int32)
    for x in range(SIDE):
        for z in range(SIDE):
            for own in range(8):
                y, c = own // 2, own % 2
                members = [2 * ((y - d) % SIDE) + e for e in (c, 1 - c) for d in SHIFTS]
                table[SIDE * x + z, own] = [
                    SIDE * ((x - f[m][0]) % SIDE) + (z - f[m][1]) % SIDE
                    for m in members
                    for f in FETCH
                ]
    return table


def gather_projection(out_proj, sent):
    first, second = [lax.ppermute(out_proj, ("seq", "exp"), fetch_pairs(f)) for f in FETCH]
    first, second, sent = lax.optimization_barrier((first, second, sent))
    up, down = [step_y(w, 1) for w in (first, second)], [step_y(w, -1) for w in (first, second)]
    near = [first, second] + up + down + [step_y(up[0], 1), step_y(down[1], -1)]
    heads = lax.dynamic_slice(
        jnp.asarray(fetched_heads()),
        (lax.axis_index("seq"), lax.axis_index("exp"), 0),
        (1, 1, 16),
    ).reshape(16)
    return heads, near + [swap(w) for w in near], sent


def shards(
    stream,
    stream_tangent,
    query_rows,
    key_rows,
    value_rows,
    query_tangent,
    key_tangent,
    value_tangent,
    out_proj,
    norm_gain,
    gate_weight,
    up_weight,
    down_weight,
    route_ids,
    route_weights,
):
    tok_dev = stream.shape[1]
    own = lax.axis_index("exp")

    sent = pack(
        [
            query_rows[0],
            key_rows[0],
            value_rows[0],
            query_tangent[0],
            key_tangent[0],
            value_tangent[0],
        ]
    )
    heads, weights, sent = gather_projection(out_proj, sent)
    received = lax.all_to_all(sent, "seq", split_axis=0, concat_axis=0, tiled=True)
    attended, attended_tangent = attend(received)
    back = lax.all_to_all(attended, "seq", split_axis=0, concat_axis=0, tiled=True)

    experts_total = lax.axis_size("exp")
    flat_ids = route_ids.reshape(-1)
    onehot = (flat_ids[:, None] == jnp.arange(experts_total, dtype=jnp.int32)[None, :]).astype(
        jnp.int32
    )
    rank_in = jnp.sum((jnp.cumsum(onehot, axis=0) - onehot) * onehot, axis=1)
    rank_in = rank_in.reshape(tok_dev, -1)
    ids = route_ids[0]
    fields = []
    for n in range(2):
        fields += [ids[:, n].astype(BF16), rank_in[:, n].astype(BF16), route_weights[0, :, n]]
    info = jnp.concatenate(
        [jnp.stack(fields), jnp.zeros((INFO - len(fields), tok_dev), BF16)], axis=0
    )

    gain = norm_gain.reshape(1, -1)
    hidden, message = project(True, heads, back, weights, stream[0], gain, info)
    back = lax.all_to_all(attended_tangent, "seq", split_axis=0, concat_axis=0, tiled=True)
    hidden_tangent, message_tangent = project(
        False, heads, back, weights, stream_tangent[0], gain, hidden
    )

    me = own.astype(jnp.int32).reshape(1)
    mats = (gate_weight[0], up_weight[0], down_weight[0])
    near = spread(message)
    near, _ = lax.optimization_barrier((near, message_tangent))
    near_tangent = spread(message_tangent)
    part, part_other, *more = expert(True, me, with_swapped(near), mats, [])
    part_other, near_tangent = lax.optimization_barrier((part_other, near_tangent))
    tokens_tangent = with_swapped(near_tangent)
    sums = chip_sums(part, part_other)
    tokens_tangent, sums = lax.optimization_barrier((tokens_tangent, sums))
    arrived = send_sums(sums)
    dpart, dpart_other = expert(False, me, tokens_tangent, mats, more)
    dpart_other, arrived = lax.optimization_barrier((dpart_other, arrived))
    layer_out = finish(hidden, sums, arrived)
    sums = chip_sums(dpart, dpart_other)
    layer_tangent = finish(hidden_tangent, sums, forward_sums(sums))
    return (layer_out[None], layer_tangent[None])


def solution(mesh):
    rows = P("exp", "seq", None)
    in_specs = (rows,) * 8 + (
        P("seq", None),
        P(),
        P("exp", None, None),
        P("exp", None, None),
        P("exp", None, None),
        rows,
        rows,
    )
    return jax.shard_map(
        shards, mesh=mesh, in_specs=in_specs, out_specs=(rows, rows), check_vma=False
    )
```

```python
import functools
import math

import jax
import jax.numpy as jnp
import numpy as np
from jax import lax
from jax.experimental import pallas as pl
from jax.experimental.pallas import tpu as pltpu
from jax.sharding import PartitionSpec as P

HEAD_DIM = 128
BF16 = jnp.bfloat16
F32 = jnp.float32
MIB = 2**20


def dot(a, b):
    return jnp.dot(a, b, preferred_element_type=F32)


def in_hbm(arrays):
    return [pltpu.with_memory_space_constraint(a, pltpu.HBM) for a in arrays]


def pack_kernel(*refs):
    ins, out = refs[:-1], refs[-1]
    heads = out.shape[0]
    for h in range(heads):
        for a, ref in enumerate(ins):
            out[h, a] = ref[:, h * HEAD_DIM : (h + 1) * HEAD_DIM]


def pack(arrays):
    rows, width = arrays[0].shape
    heads = width // HEAD_DIM
    step = 4
    return pl.pallas_call(
        pack_kernel,
        grid=(heads // step,),
        out_shape=jax.ShapeDtypeStruct((heads, len(arrays), rows, HEAD_DIM), BF16),
        in_specs=[pl.BlockSpec((rows, step * HEAD_DIM), lambda i: (0, i))] * len(arrays),
        out_specs=pl.BlockSpec((step, len(arrays), rows, HEAD_DIM), lambda i: (i, 0, 0, 0)),
        cost_estimate=pl.CostEstimate(
            flops=0, bytes_accessed=4 * len(arrays) * rows * width, transcendentals=0
        ),
        name="pack_heads",
    )(*arrays)


KEYS = 512


def attend_kernel(blocks, r_ref, o_ref, t_ref, kt, vv):
    sources, _, rows, _ = r_ref.shape
    i = pl.program_id(0)

    @pl.when(i == 0)
    def _():
        for s in range(sources):
            at = slice(s * rows, (s + 1) * rows)
            kt[:HEAD_DIM, at] = r_ref[s, 1].T
            kt[HEAD_DIM:, at] = r_ref[s, 4].T
            vv[at, :HEAD_DIM] = r_ref[s, 2]
            vv[at, HEAD_DIM:] = r_ref[s, 5]

    scale = 1.0 / math.sqrt(HEAD_DIM)
    q = r_ref[pl.ds(i * blocks, blocks), 0].reshape(blocks * rows, HEAD_DIM)
    dq = r_ref[pl.ds(i * blocks, blocks), 3].reshape(blocks * rows, HEAD_DIM)
    s = dot(q, kt[:HEAD_DIM])
    dqq = jnp.concatenate([dq, q], axis=1)
    factor = scale * math.log2(math.e)
    peak = jnp.max(s, axis=-1, keepdims=True) * factor
    total = row_sum = both = wv = 0.0
    for c in range(0, s.shape[1], KEYS):
        at = slice(c, c + KEYS)
        e = jnp.exp2(s[:, at] * factor - peak)
        total = total + jnp.sum(e, axis=-1, keepdims=True)
        w = e * dot(dqq, kt[:, at])
        row_sum = row_sum + jnp.sum(w, axis=-1, keepdims=True)
        both = both + dot(e.astype(BF16), vv[at])
        wv = wv + dot(w.astype(BF16), vv[at, :HEAD_DIM])
    inv = 1.0 / total
    att = both[:, :HEAD_DIM] * inv
    tan = (wv * scale + both[:, HEAD_DIM:]) * inv - (row_sum * (inv * scale)) * att
    o_ref[...] = att.astype(BF16).reshape(blocks, rows, HEAD_DIM)
    t_ref[...] = tan.astype(BF16).reshape(blocks, rows, HEAD_DIM)


def attend(received, blocks=4):
    sources, _, rows, _ = received.shape
    seq_len = sources * rows
    return pl.pallas_call(
        functools.partial(attend_kernel, blocks),
        grid=(sources // blocks,),
        out_shape=(pltpu.HBM((sources, rows, HEAD_DIM), BF16),) * 2,
        in_specs=[pl.BlockSpec(received.shape, lambda i: (0, 0, 0, 0))],
        out_specs=(pl.BlockSpec((blocks, rows, HEAD_DIM), lambda i: (i, 0, 0)),) * 2,
        scratch_shapes=[
            pltpu.VMEM((2 * HEAD_DIM, seq_len), BF16),
            pltpu.VMEM((seq_len, 2 * HEAD_DIM), BF16),
        ],
        compiler_params=pltpu.CompilerParams(vmem_limit_bytes=32 * MIB),
        cost_estimate=pl.CostEstimate(
            flops=16 * seq_len * seq_len * HEAD_DIM,
            bytes_accessed=16 * seq_len * HEAD_DIM,
            transcendentals=seq_len * seq_len,
        ),
        name="attend_head",
    )(received)


def project_kernel(primal, heads, *refs):
    w_refs, refs = refs[:16], refs[16:]
    s_in, a_ref, g_ref, more, h_ref, m_ref, x, wv, sem, s_ref, asem = refs
    rows, width = h_ref.shape
    loads = [
        pltpu.make_async_copy(ref, wv.at[n * HEAD_DIM : (n + 1) * HEAD_DIM], sem.at[n])
        for n, ref in enumerate(w_refs)
    ]
    stream_load = pltpu.make_async_copy(s_in, s_ref, asem)
    for load in loads + [stream_load]:
        load.start()
    for h in range(a_ref.shape[0]):
        x[:, h * HEAD_DIM : (h + 1) * HEAD_DIM] = a_ref[heads[h]]
    half, tile = width // 2, 512
    stream_load.wait()
    for part in range(2):
        for load in loads[8 * part : 8 * part + 8]:
            load.wait()
        k = slice(part * half, (part + 1) * half)
        for n in range(0, width, tile):
            at = slice(n, n + tile)
            before = s_ref[:, at].astype(F32) if part == 0 else h_ref[:, at]
            h_ref[:, at] = before + dot(x[:, k], wv[k, at])
    gain = g_ref[...].astype(F32)
    if primal:
        hid = h_ref[...]
        inverse = lax.rsqrt(jnp.mean(hid * hid, axis=-1, keepdims=True) + 1e-06)
        normed = (hid * inverse * gain).astype(BF16)
        middle, info = rows // 2, more.shape[0]
        m_ref[:middle] = normed[:middle]
        m_ref[middle : middle + info] = jnp.zeros((info, width), BF16)
        m_ref[middle : middle + info, : more.shape[1]] = more[...]
        m_ref[middle + info :] = normed[middle:]
    else:
        hid, tan = more[...], h_ref[...]
        inverse = lax.rsqrt(jnp.mean(hid * hid, axis=-1, keepdims=True) + 1e-06)
        cross = jnp.mean(hid * tan, axis=-1, keepdims=True)
        m_ref[...] = (
            gain * (tan * inverse - hid * (inverse * inverse * inverse) * cross)
        ).astype(BF16)


def project(primal, heads, attended, weights, stream, gain, more):
    rows, width = stream.shape
    vmem = pl.BlockSpec(memory_space=pltpu.VMEM)
    hbm = pl.BlockSpec(memory_space=pltpu.HBM)
    sent = rows + more.shape[0] if primal else rows
    return pl.pallas_call(
        functools.partial(project_kernel, primal),
        out_shape=(
            jax.ShapeDtypeStruct((rows, width), F32),
            jax.ShapeDtypeStruct((sent, width), BF16),
        ),
        in_specs=[pl.BlockSpec(memory_space=pltpu.SMEM)]
        + [hbm] * 17
        + [vmem] * 3,
        out_specs=(vmem,) * 2,
        scratch_shapes=[
            pltpu.VMEM((rows, width), BF16),
            pltpu.VMEM((width, width), BF16),
            pltpu.SemaphoreType.DMA((16,)),
            pltpu.VMEM((rows, width), BF16),
            pltpu.SemaphoreType.DMA,
        ],
        compiler_params=pltpu.CompilerParams(vmem_limit_bytes=32 * MIB),
        cost_estimate=pl.CostEstimate(
            flops=2 * rows * width * width, bytes_accessed=3 * width * width, transcendentals=0
        ),
        name="project_primal" if primal else "project_tangent",
    )(heads, *in_hbm([*weights, stream]), attended, gain, more)


SLOTS = 64
INFO = 16
TILES = (512, 512, 384)
COLS = 1024


def expert_kernel(primal, rows, *refs):
    it = iter(refs)
    take = lambda n: [next(it) for _ in range(n)]
    (me,) = take(1)
    messages = take(8)
    wb, db = take(2)
    if primal:
        own, other, cb, disp, comb = take(5)
    else:
        cb, disp, comb = take(3)
        own, other = take(2)
    mb, xs, hid, ct, msem = take(5)
    tokens, width = own.shape[1:]
    steps, cols = len(TILES), width // COLS
    starts = [sum(TILES[:n]) for n in range(steps)]
    loads = [pltpu.make_async_copy(a, b, msem.at[n]) for n, (a, b) in enumerate(zip(messages, [mb.at[k] for k in range(8)]))]
    for load in loads:
        load.start()

    ct[...] = jnp.zeros(ct.shape, BF16)
    for load in loads:
        load.wait()

    half = tokens // 2
    none = jnp.zeros((SLOTS, tokens), F32)

    def diagonal(first, second):
        return jnp.concatenate(
            [
                jnp.concatenate([first, none], axis=1),
                jnp.concatenate([none, second], axis=1),
            ],
            axis=0,
        )

    def slots_of(k):
        if not primal:
            return disp[k].astype(F32), comb[k].astype(F32), mb[k]
        info = mb[k, half : half + INFO, :tokens].astype(F32)
        slot = lax.broadcasted_iota(jnp.int32, (SLOTS, tokens), 0).astype(F32)
        mine = me[0].astype(F32)
        d, c = none, none
        for n in range(2):
            hit = (info[3 * n : 3 * n + 1] == mine) & (info[3 * n + 1 : 3 * n + 2] == slot)
            d = d + jnp.where(hit, 1.0, 0.0)
            c = c + jnp.where(hit, info[3 * n + 2 : 3 * n + 3], 0.0)
        disp[k] = d.astype(BF16)
        comb[k] = c.astype(BF16)
        return d, c, jnp.concatenate([mb[k, :half], mb[k, half + INFO :]], axis=0)

    def pair_step(p, carry):
        d0, c0, tok0 = slots_of(2 * p)
        d1, c1, tok1 = slots_of(2 * p + 1)
        q = p % 2
        rows_at = pl.ds(pl.multiple_of(q * 2 * tokens, 2 * tokens), 2 * tokens)
        cols_at = pl.ds(pl.multiple_of(q * 2 * SLOTS, 2 * SLOTS), 2 * SLOTS)
        ct[p // 2, rows_at, cols_at] = diagonal(c0, c1).T.astype(BF16)
        at = pl.ds(pl.multiple_of(p * 2 * SLOTS, 2 * SLOTS), 2 * SLOTS)
        xs[at] = dot(
            diagonal(d0, d1).astype(BF16), jnp.concatenate([tok0, tok1], axis=0)
        ).astype(BF16)
        return carry

    lax.fori_loop(0, 4, pair_step, 0)

    def finish(f, both):
        tile = TILES[f]
        at = slice(starts[f], starts[f] + tile)
        g, u = both[:, :tile], both[:, tile:]
        if primal:
            sig = 0.5 * jnp.tanh(0.5 * g) + 0.5
            act = g * sig
            hid[:, at] = (act * u).astype(BF16)
            cb[0, :, at] = ((sig + act - act * sig) * u).astype(BF16)
            cb[1, :, at] = act.astype(BF16)
        else:
            hid[:, at] = (
                cb[0, :, at].astype(F32) * g + cb[1, :, at].astype(F32) * u
            ).astype(BF16)

    before = None
    for f in range(steps):
        both = dot(xs[...], wb[f, :, : 2 * TILES[f]])
        if f > 0:
            finish(f - 1, before)
        before = both
    finish(steps - 1, before)
    for j in range(cols):
        at = slice(j * COLS, (j + 1) * COLS)
        out = dot(hid[...], db[j]).astype(BF16)
        for quad in range(2):
            part = dot(ct[quad], out[quad * 4 * SLOTS : (quad + 1) * 4 * SLOTS]).astype(BF16)
            for member in range(4):
                k = quad * 4 + member
                (own, other)[k % 2][k // 2, :, at] = part[member * tokens : (member + 1) * tokens]


def load_kernel(gate, up, down, wb, db, done, wsem, dsem):
    loads = []
    start = 0
    for f, tile in enumerate(TILES):
        at = slice(start, start + tile)
        start += tile
        loads += [
            pltpu.make_async_copy(gate.at[:, at], wb.at[f, :, :tile], wsem.at[0, f]),
            pltpu.make_async_copy(up.at[:, at], wb.at[f, :, tile : 2 * tile], wsem.at[1, f]),
        ]
    for j in range(db.shape[0]):
        at = slice(j * COLS, (j + 1) * COLS)
        loads.append(pltpu.make_async_copy(down.at[:, at], db.at[j], dsem.at[j]))
    for load in loads:
        load.start()
    for load in loads:
        load.wait()
    done[...] = jnp.zeros(done.shape, F32)


def load_expert(gate, up, down):
    width, ff = gate.shape
    vmem = pl.BlockSpec(memory_space=pltpu.VMEM)
    return pl.pallas_call(
        load_kernel,
        out_shape=(
            pltpu.VMEM((len(TILES), width, 2 * TILES[0]), BF16),
            pltpu.VMEM((width // COLS, ff, COLS), BF16),
            jax.ShapeDtypeStruct((8, 128), F32),
        ),
        in_specs=[pl.BlockSpec(memory_space=pl.ANY)] * 3,
        out_specs=(vmem,) * 3,
        scratch_shapes=[
            pltpu.SemaphoreType.DMA((2, len(TILES))),
            pltpu.SemaphoreType.DMA((width // COLS,)),
        ],
        compiler_params=pltpu.CompilerParams(vmem_limit_bytes=4 * MIB),
        cost_estimate=pl.CostEstimate(
            flops=0, bytes_accessed=12 * width * ff, transcendentals=0
        ),
        name="load_expert",
    )(*in_hbm([gate, up, down]))


def expert(primal, me, messages, weights, more):
    wb, db, *more = [
        pltpu.with_memory_space_constraint(a, pltpu.VMEM) for a in [*weights, *more[:1]]
    ] + more[1:]
    width, ff = wb.shape[1], db.shape[1]
    tokens = more[1].shape[2] if more else messages[0].shape[0] - INFO
    rows = messages[0].shape[0]
    slots = 8 * SLOTS
    vmem = pl.BlockSpec(memory_space=pltpu.VMEM)
    anywhere = pl.BlockSpec(memory_space=pl.ANY)
    out_shape = [pltpu.VMEM((4, tokens, width), BF16)] * 2
    out_specs = [vmem] * 2
    scratch = [
        pltpu.VMEM((8, rows, width), BF16),
        pltpu.VMEM((slots, width), BF16),
        pltpu.VMEM((slots, ff), BF16),
        pltpu.VMEM((2, 4 * tokens, 4 * SLOTS), BF16),
        pltpu.SemaphoreType.DMA((8,)),
    ]
    if primal:
        out_shape += [
            pltpu.VMEM((2, slots, ff), BF16),
            jax.ShapeDtypeStruct((8, SLOTS, tokens), BF16),
            jax.ShapeDtypeStruct((8, SLOTS, tokens), BF16),
        ]
        out_specs += [vmem, vmem, vmem]
    return pl.pallas_call(
        functools.partial(expert_kernel, primal, rows),
        out_shape=tuple(out_shape),
        in_specs=[pl.BlockSpec(memory_space=pltpu.SMEM)]
        + [anywhere] * 8
        + [vmem] * 2
        + [vmem] * len(more),
        out_specs=tuple(out_specs),
        scratch_shapes=scratch,
        compiler_params=pltpu.CompilerParams(vmem_limit_bytes=24 * MIB),
        cost_estimate=pl.CostEstimate(
            flops=0 if primal else 6 * slots * width * ff,
            bytes_accessed=0 if primal else 6 * width * ff + 24 * tokens * width,
            transcendentals=0 if primal else slots * ff,
        ),
        name="expert_primal" if primal else "expert_tangent",
    )(me, *in_hbm(messages), wb, db, *more)


def step_y(x, distance):
    chips = lax.axis_size("exp") // 2
    pairs = [
        (2 * y + c, 2 * ((y + distance) % chips) + c) for y in range(chips) for c in range(2)
    ]
    return lax.ppermute(x, "exp", pairs)


def swap(x):
    count = lax.axis_size("exp")
    return lax.ppermute(x, "exp", [(n, n ^ 1) for n in range(count)])


def spread(x):
    return [x] + [step_y(x, n) for n in SHIFTS[1:]]


def with_swapped(near):
    return [m for one in near for m in (one, swap(one))]


def chip_sums(own, other):
    got = swap(other)
    sums = [own[n].astype(F32) + got[n].astype(F32) for n in range(4)]
    return sums[:1] + [one.astype(BF16) for one in sums[1:]]


def send_first(sums):
    here, before, after, far = sums
    half = far.shape[0] // 2
    via = [step_y(far[:half], 1), step_y(far[half:], -1)]
    free = [step_y(after[half:], 1), step_y(before[:half], -1)]
    return via, free


def added(sums, via):
    here, before, after, far = sums
    half = far.shape[0] // 2
    add = lambda a, b: (a.astype(F32) + b.astype(F32)).astype(BF16)
    return [add(after[:half], via[0]), add(before[half:], via[1])]


def send_last(ahead, back):
    return [step_y(ahead, 1), step_y(back, -1)]


def joined(free, late):
    return [
        jnp.concatenate([late[0], free[0]], axis=0),
        jnp.concatenate([free[1], late[1]], axis=0),
    ]


def finish(base, sums, arrived):
    here = sums[0]
    for one in arrived:
        here = here + one.astype(F32)
    return (base + here).astype(BF16)


SHIFTS = (0, 1, -1, 2)


FETCH = (
    ((2, 2), (1, 1), (-1, 0), (2, 1), (1, 0), (2, -1), (2, 0), (0, 2)),
    ((0, 0), (-1, -1), (1, 2), (0, -1), (-1, 2), (0, 1), (1, -1), (-1, 1)),
)
SIDE = 4


def fetch_pairs(offsets):
    return [
        (
            (SIDE * x + z) * 8 + m,
            (SIDE * ((x + offsets[m][0]) % SIDE) + (z + offsets[m][1]) % SIDE) * 8 + m,
        )
        for x in range(SIDE)
        for z in range(SIDE)
        for m in range(8)
    ]


def fetched_heads():
    table = np.zeros((16, 8, 16), np.int32)
    for x in range(SIDE):
        for z in range(SIDE):
            for own in range(8):
                y, c = own // 2, own % 2
                members = [2 * ((y - d) % SIDE) + e for e in (c, 1 - c) for d in SHIFTS]
                table[SIDE * x + z, own] = [
                    SIDE * ((x - f[m][0]) % SIDE) + (z - f[m][1]) % SIDE
                    for m in members
                    for f in FETCH
                ]
    return table


def gather_projection(out_proj, sent):
    first, second = [lax.ppermute(out_proj, ("seq", "exp"), fetch_pairs(f)) for f in FETCH]
    first, second, sent = lax.optimization_barrier((first, second, sent))
    up, down = [step_y(w, 1) for w in (first, second)], [step_y(w, -1) for w in (first, second)]
    near = [first, second] + up + down + [step_y(up[0], 1), step_y(down[1], -1)]
    heads = lax.dynamic_slice(
        jnp.asarray(fetched_heads()),
        (lax.axis_index("seq"), lax.axis_index("exp"), 0),
        (1, 1, 16),
    ).reshape(16)
    return heads, near + [swap(w) for w in near], sent


def shards(
    stream,
    stream_tangent,
    query_rows,
    key_rows,
    value_rows,
    query_tangent,
    key_tangent,
    value_tangent,
    out_proj,
    norm_gain,
    gate_weight,
    up_weight,
    down_weight,
    route_ids,
    route_weights,
):
    tok_dev = stream.shape[1]
    own = lax.axis_index("exp")

    sent = pack(
        [
            query_rows[0],
            key_rows[0],
            value_rows[0],
            query_tangent[0],
            key_tangent[0],
            value_tangent[0],
        ]
    )
    heads, weights, sent = gather_projection(out_proj, sent)
    received = lax.all_to_all(sent, "seq", split_axis=0, concat_axis=0, tiled=True)
    attended, attended_tangent = attend(received)
    back = lax.all_to_all(attended, "seq", split_axis=0, concat_axis=0, tiled=True)

    experts_total = lax.axis_size("exp")
    flat_ids = route_ids.reshape(-1)
    onehot = (flat_ids[:, None] == jnp.arange(experts_total, dtype=jnp.int32)[None, :]).astype(
        jnp.int32
    )
    rank_in = jnp.sum((jnp.cumsum(onehot, axis=0) - onehot) * onehot, axis=1)
    rank_in = rank_in.reshape(tok_dev, -1)
    ids = route_ids[0]
    fields = []
    for n in range(2):
        fields += [ids[:, n].astype(BF16), rank_in[:, n].astype(BF16), route_weights[0, :, n]]
    info = jnp.concatenate(
        [jnp.stack(fields), jnp.zeros((INFO - len(fields), tok_dev), BF16)], axis=0
    )

    gain = norm_gain.reshape(1, -1)
    hidden, message = project(True, heads, back, weights, stream[0], gain, info)
    back = lax.all_to_all(attended_tangent, "seq", split_axis=0, concat_axis=0, tiled=True)
    hidden_tangent, message_tangent = project(
        False, heads, back, weights, stream_tangent[0], gain, hidden
    )

    me = own.astype(jnp.int32).reshape(1)
    near = spread(message)
    *mats, loaded = load_expert(gate_weight[0], up_weight[0], down_weight[0])
    near, _, _ = lax.optimization_barrier((near, message_tangent, loaded))
    near_tangent = spread(message_tangent)
    part, part_other, *more = expert(True, me, with_swapped(near), mats, [])
    part_other, near_tangent = lax.optimization_barrier((part_other, near_tangent))
    tokens_tangent = with_swapped(near_tangent)
    sums = chip_sums(part, part_other)
    tokens_tangent, sums = lax.optimization_barrier((tokens_tangent, sums))
    via, free = send_first(sums)
    dpart, dpart_other = expert(False, me, tokens_tangent, mats, more)
    dpart_other, via, free = lax.optimization_barrier((dpart_other, via, free))
    late = send_last(*added(sums, via))
    dsums = chip_sums(dpart, dpart_other)
    dvia, dfree = send_first(dsums)
    dlast = added(dsums, dvia)
    dlast, late = lax.optimization_barrier((dlast, late))
    layer_out = finish(hidden, sums, joined(free, late))
    layer_tangent = finish(hidden_tangent, dsums, joined(dfree, send_last(*dlast)))
    return (layer_out[None], layer_tangent[None])


def solution(mesh):
    rows = P("exp", "seq", None)
    in_specs = (rows,) * 8 + (
        P("seq", None),
        P(),
        P("exp", None, None),
        P("exp", None, None),
        P("exp", None, None),
        rows,
        rows,
    )
    return jax.shard_map(
        shards, mesh=mesh, in_specs=in_specs, out_specs=(rows, rows), check_vma=False
    )
```

```python
import functools
import math

import jax
import jax.numpy as jnp
import numpy as np
from jax import lax
from jax.experimental import pallas as pl
from jax.experimental.pallas import tpu as pltpu
from jax.sharding import PartitionSpec as P

HEAD_DIM = 128
BF16 = jnp.bfloat16
F32 = jnp.float32
MIB = 2**20


def dot(a, b):
    return jnp.dot(a, b, preferred_element_type=F32)


def in_hbm(arrays):
    return [pltpu.with_memory_space_constraint(a, pltpu.HBM) for a in arrays]


def pack_kernel(*refs):
    ins, out = refs[:-1], refs[-1]
    heads = out.shape[0]
    for h in range(heads):
        for a, ref in enumerate(ins):
            out[h, a] = ref[:, h * HEAD_DIM : (h + 1) * HEAD_DIM]


def pack(arrays):
    rows, width = arrays[0].shape
    heads = width // HEAD_DIM
    step = 4
    return pl.pallas_call(
        pack_kernel,
        grid=(heads // step,),
        out_shape=jax.ShapeDtypeStruct((heads, len(arrays), rows, HEAD_DIM), BF16),
        in_specs=[pl.BlockSpec((rows, step * HEAD_DIM), lambda i: (0, i))] * len(arrays),
        out_specs=pl.BlockSpec((step, len(arrays), rows, HEAD_DIM), lambda i: (i, 0, 0, 0)),
        cost_estimate=pl.CostEstimate(
            flops=0, bytes_accessed=4 * len(arrays) * rows * width, transcendentals=0
        ),
        name="pack_heads",
    )(*arrays)


KEYS = 512


def attend_kernel(blocks, r_ref, o_ref, t_ref, kt, vv):
    sources, _, rows, _ = r_ref.shape
    i = pl.program_id(0)

    @pl.when(i == 0)
    def _():
        for s in range(sources):
            at = slice(s * rows, (s + 1) * rows)
            kt[:HEAD_DIM, at] = r_ref[s, 1].T
            kt[HEAD_DIM:, at] = r_ref[s, 4].T
            vv[at, :HEAD_DIM] = r_ref[s, 2]
            vv[at, HEAD_DIM:] = r_ref[s, 5]

    scale = 1.0 / math.sqrt(HEAD_DIM)
    q = r_ref[pl.ds(i * blocks, blocks), 0].reshape(blocks * rows, HEAD_DIM)
    dq = r_ref[pl.ds(i * blocks, blocks), 3].reshape(blocks * rows, HEAD_DIM)
    s = dot(q, kt[:HEAD_DIM])
    dqq = jnp.concatenate([dq, q], axis=1)
    factor = scale * math.log2(math.e)
    peak = jnp.max(s, axis=-1, keepdims=True) * factor
    total = row_sum = both = wv = 0.0
    for c in range(0, s.shape[1], KEYS):
        at = slice(c, c + KEYS)
        e = jnp.exp2(s[:, at] * factor - peak)
        total = total + jnp.sum(e, axis=-1, keepdims=True)
        w = e * dot(dqq, kt[:, at])
        row_sum = row_sum + jnp.sum(w, axis=-1, keepdims=True)
        both = both + dot(e.astype(BF16), vv[at])
        wv = wv + dot(w.astype(BF16), vv[at, :HEAD_DIM])
    inv = 1.0 / total
    att = both[:, :HEAD_DIM] * inv
    tan = (wv * scale + both[:, HEAD_DIM:]) * inv - (row_sum * (inv * scale)) * att
    o_ref[...] = att.astype(BF16).reshape(blocks, rows, HEAD_DIM)
    t_ref[...] = tan.astype(BF16).reshape(blocks, rows, HEAD_DIM)


def attend(received, blocks=4):
    sources, _, rows, _ = received.shape
    seq_len = sources * rows
    return pl.pallas_call(
        functools.partial(attend_kernel, blocks),
        grid=(sources // blocks,),
        out_shape=(pltpu.HBM((sources, rows, HEAD_DIM), BF16),) * 2,
        in_specs=[pl.BlockSpec(received.shape, lambda i: (0, 0, 0, 0))],
        out_specs=(pl.BlockSpec((blocks, rows, HEAD_DIM), lambda i: (i, 0, 0)),) * 2,
        scratch_shapes=[
            pltpu.VMEM((2 * HEAD_DIM, seq_len), BF16),
            pltpu.VMEM((seq_len, 2 * HEAD_DIM), BF16),
        ],
        compiler_params=pltpu.CompilerParams(vmem_limit_bytes=32 * MIB),
        cost_estimate=pl.CostEstimate(
            flops=16 * seq_len * seq_len * HEAD_DIM,
            bytes_accessed=16 * seq_len * HEAD_DIM,
            transcendentals=seq_len * seq_len,
        ),
        name="attend_head",
    )(received)


def project_kernel(primal, heads, *refs):
    w_refs, refs = refs[:16], refs[16:]
    s_in, a_ref, g_ref, more, h_ref, m_ref, x, wv, sem, s_ref, asem = refs
    rows, width = h_ref.shape
    loads = [
        pltpu.make_async_copy(ref, wv.at[n * HEAD_DIM : (n + 1) * HEAD_DIM], sem.at[n])
        for n, ref in enumerate(w_refs)
    ]
    stream_load = pltpu.make_async_copy(s_in, s_ref, asem)
    for load in loads + [stream_load]:
        load.start()
    for h in range(a_ref.shape[0]):
        x[:, h * HEAD_DIM : (h + 1) * HEAD_DIM] = a_ref[heads[h]]
    half, tile = width // 2, 512
    stream_load.wait()
    for part in range(2):
        for load in loads[8 * part : 8 * part + 8]:
            load.wait()
        k = slice(part * half, (part + 1) * half)
        for n in range(0, width, tile):
            at = slice(n, n + tile)
            before = s_ref[:, at].astype(F32) if part == 0 else h_ref[:, at]
            h_ref[:, at] = before + dot(x[:, k], wv[k, at])
    gain = g_ref[...].astype(F32)
    if primal:
        hid = h_ref[...]
        inverse = lax.rsqrt(jnp.mean(hid * hid, axis=-1, keepdims=True) + 1e-06)
        normed = (hid * inverse * gain).astype(BF16)
        middle, info = rows // 2, more.shape[0]
        m_ref[:middle] = normed[:middle]
        m_ref[middle : middle + info] = jnp.zeros((info, width), BF16)
        m_ref[middle : middle + info, : more.shape[1]] = more[...]
        m_ref[middle + info :] = normed[middle:]
    else:
        hid, tan = more[...], h_ref[...]
        inverse = lax.rsqrt(jnp.mean(hid * hid, axis=-1, keepdims=True) + 1e-06)
        cross = jnp.mean(hid * tan, axis=-1, keepdims=True)
        m_ref[...] = (
            gain * (tan * inverse - hid * (inverse * inverse * inverse) * cross)
        ).astype(BF16)


def project(primal, heads, attended, weights, stream, gain, more):
    rows, width = stream.shape
    vmem = pl.BlockSpec(memory_space=pltpu.VMEM)
    hbm = pl.BlockSpec(memory_space=pltpu.HBM)
    sent = rows + more.shape[0] if primal else rows
    return pl.pallas_call(
        functools.partial(project_kernel, primal),
        out_shape=(
            jax.ShapeDtypeStruct((rows, width), F32),
            jax.ShapeDtypeStruct((sent, width), BF16),
        ),
        in_specs=[pl.BlockSpec(memory_space=pltpu.SMEM)]
        + [hbm] * 17
        + [vmem] * 3,
        out_specs=(vmem,) * 2,
        scratch_shapes=[
            pltpu.VMEM((rows, width), BF16),
            pltpu.VMEM((width, width), BF16),
            pltpu.SemaphoreType.DMA((16,)),
            pltpu.VMEM((rows, width), BF16),
            pltpu.SemaphoreType.DMA,
        ],
        compiler_params=pltpu.CompilerParams(vmem_limit_bytes=32 * MIB),
        cost_estimate=pl.CostEstimate(
            flops=2 * rows * width * width, bytes_accessed=3 * width * width, transcendentals=0
        ),
        name="project_primal" if primal else "project_tangent",
    )(heads, *in_hbm([*weights, stream]), attended, gain, more)


SLOTS = 64
INFO = 16
TILES = (512, 512, 384)
COLS = 1024


def expert_kernel(primal, rows, *refs):
    it = iter(refs)
    take = lambda n: [next(it) for _ in range(n)]
    (me,) = take(1)
    messages = take(8)
    wb, db = take(2)
    if primal:
        take(1)
        own, other, cb, disp, comb = take(5)
    else:
        cb, disp, comb = take(3)
        own, other = take(2)
    mb, xs, hid, ct, msem = take(5)
    tokens, width = own.shape[1:]
    steps, cols = len(TILES), width // COLS
    starts = [sum(TILES[:n]) for n in range(steps)]
    loads = [pltpu.make_async_copy(a, b, msem.at[n]) for n, (a, b) in enumerate(zip(messages, [mb.at[k] for k in range(8)]))]
    for load in loads:
        load.start()

    ct[...] = jnp.zeros(ct.shape, BF16)
    for load in loads:
        load.wait()

    half = tokens // 2
    none = jnp.zeros((SLOTS, tokens), F32)

    def diagonal(first, second):
        return jnp.concatenate(
            [
                jnp.concatenate([first, none], axis=1),
                jnp.concatenate([none, second], axis=1),
            ],
            axis=0,
        )

    def slots_of(k):
        if not primal:
            return disp[k].astype(F32), comb[k].astype(F32), mb[k]
        info = mb[k, half : half + INFO, :tokens].astype(F32)
        slot = lax.broadcasted_iota(jnp.int32, (SLOTS, tokens), 0).astype(F32)
        mine = me[0].astype(F32)
        d, c = none, none
        for n in range(2):
            hit = (info[3 * n : 3 * n + 1] == mine) & (info[3 * n + 1 : 3 * n + 2] == slot)
            d = d + jnp.where(hit, 1.0, 0.0)
            c = c + jnp.where(hit, info[3 * n + 2 : 3 * n + 3], 0.0)
        disp[k] = d.astype(BF16)
        comb[k] = c.astype(BF16)
        return d, c, jnp.concatenate([mb[k, :half], mb[k, half + INFO :]], axis=0)

    def pair_step(p, carry):
        d0, c0, tok0 = slots_of(2 * p)
        d1, c1, tok1 = slots_of(2 * p + 1)
        q = p % 2
        rows_at = pl.ds(pl.multiple_of(q * 2 * tokens, 2 * tokens), 2 * tokens)
        cols_at = pl.ds(pl.multiple_of(q * 2 * SLOTS, 2 * SLOTS), 2 * SLOTS)
        ct[p // 2, rows_at, cols_at] = diagonal(c0, c1).T.astype(BF16)
        at = pl.ds(pl.multiple_of(p * 2 * SLOTS, 2 * SLOTS), 2 * SLOTS)
        xs[at] = dot(
            diagonal(d0, d1).astype(BF16), jnp.concatenate([tok0, tok1], axis=0)
        ).astype(BF16)
        return carry

    lax.fori_loop(0, 4, pair_step, 0)

    def finish(f, both):
        tile = TILES[f]
        at = slice(starts[f], starts[f] + tile)
        g, u = both[:, :tile], both[:, tile:]
        if primal:
            sig = 0.5 * jnp.tanh(0.5 * g) + 0.5
            act = g * sig
            hid[:, at] = (act * u).astype(BF16)
            cb[0, :, at] = ((sig + act - act * sig) * u).astype(BF16)
            cb[1, :, at] = act.astype(BF16)
        else:
            hid[:, at] = (
                cb[0, :, at].astype(F32) * g + cb[1, :, at].astype(F32) * u
            ).astype(BF16)

    before = None
    for f in range(steps):
        both = dot(xs[...], wb[f, :, : 2 * TILES[f]])
        if f > 0:
            finish(f - 1, before)
        before = both
    finish(steps - 1, before)
    for j in range(cols):
        at = slice(j * COLS, (j + 1) * COLS)
        out = dot(hid[...], db[j]).astype(BF16)
        for quad in range(2):
            part = dot(ct[quad], out[quad * 4 * SLOTS : (quad + 1) * 4 * SLOTS]).astype(BF16)
            for member in range(4):
                k = quad * 4 + member
                (own, other)[k % 2][k // 2, :, at] = part[member * tokens : (member + 1) * tokens]


def load_kernel(gate, up, down, wb, db, done, wsem, dsem):
    loads = []
    start = 0
    for f, tile in enumerate(TILES):
        at = slice(start, start + tile)
        start += tile
        loads += [
            pltpu.make_async_copy(gate.at[:, at], wb.at[f, :, :tile], wsem.at[0, f]),
            pltpu.make_async_copy(up.at[:, at], wb.at[f, :, tile : 2 * tile], wsem.at[1, f]),
        ]
    for j in range(db.shape[0]):
        at = slice(j * COLS, (j + 1) * COLS)
        loads.append(pltpu.make_async_copy(down.at[:, at], db.at[j], dsem.at[j]))
    for load in loads:
        load.start()
    for load in loads:
        load.wait()
    done[...] = jnp.zeros(done.shape, F32)


def load_expert(gate, up, down):
    width, ff = gate.shape
    vmem = pl.BlockSpec(memory_space=pltpu.VMEM)
    return pl.pallas_call(
        load_kernel,
        out_shape=(
            pltpu.VMEM((len(TILES), width, 2 * TILES[0]), BF16),
            pltpu.VMEM((width // COLS, ff, COLS), BF16),
            jax.ShapeDtypeStruct((8, 128), F32),
        ),
        in_specs=[pl.BlockSpec(memory_space=pl.ANY)] * 3,
        out_specs=(vmem,) * 3,
        scratch_shapes=[
            pltpu.SemaphoreType.DMA((2, len(TILES))),
            pltpu.SemaphoreType.DMA((width // COLS,)),
        ],
        compiler_params=pltpu.CompilerParams(vmem_limit_bytes=4 * MIB),
        cost_estimate=pl.CostEstimate(
            flops=0, bytes_accessed=12 * width * ff, transcendentals=0
        ),
        name="load_expert",
    )(*in_hbm([gate, up, down]))


def expert(primal, me, messages, weights, more, *after):
    wb, db, *more = [
        pltpu.with_memory_space_constraint(a, pltpu.VMEM) for a in [*weights, *more[:1]]
    ] + more[1:]
    width, ff = wb.shape[1], db.shape[1]
    tokens = more[1].shape[2] if more else messages[0].shape[0] - INFO
    rows = messages[0].shape[0]
    slots = 8 * SLOTS
    vmem = pl.BlockSpec(memory_space=pltpu.VMEM)
    anywhere = pl.BlockSpec(memory_space=pl.ANY)
    out_shape = [pltpu.VMEM((4, tokens, width), BF16)] * 2
    out_specs = [vmem] * 2
    scratch = [
        pltpu.VMEM((8, rows, width), BF16),
        pltpu.VMEM((slots, width), BF16),
        pltpu.VMEM((slots, ff), BF16),
        pltpu.VMEM((2, 4 * tokens, 4 * SLOTS), BF16),
        pltpu.SemaphoreType.DMA((8,)),
    ]
    if primal:
        out_shape += [
            pltpu.VMEM((2, slots, ff), BF16),
            jax.ShapeDtypeStruct((8, SLOTS, tokens), BF16),
            jax.ShapeDtypeStruct((8, SLOTS, tokens), BF16),
        ]
        out_specs += [vmem, vmem, vmem]
    return pl.pallas_call(
        functools.partial(expert_kernel, primal, rows),
        out_shape=tuple(out_shape),
        in_specs=[pl.BlockSpec(memory_space=pltpu.SMEM)]
        + [anywhere] * 8
        + [vmem] * 2
        + [vmem] * (len(more) + len(after)),
        out_specs=tuple(out_specs),
        scratch_shapes=scratch,
        compiler_params=pltpu.CompilerParams(vmem_limit_bytes=24 * MIB),
        cost_estimate=pl.CostEstimate(
            flops=0 if primal else 6 * slots * width * ff,
            bytes_accessed=0 if primal else 6 * width * ff + 24 * tokens * width,
            transcendentals=0 if primal else slots * ff,
        ),
        name="expert_primal" if primal else "expert_tangent",
    )(me, *in_hbm(messages), wb, db, *more, *after)


def step_y(x, distance):
    chips = lax.axis_size("exp") // 2
    pairs = [
        (2 * y + c, 2 * ((y + distance) % chips) + c) for y in range(chips) for c in range(2)
    ]
    return lax.ppermute(x, "exp", pairs)


def swap(x):
    count = lax.axis_size("exp")
    return lax.ppermute(x, "exp", [(n, n ^ 1) for n in range(count)])


def spread(x):
    return [x] + [step_y(x, n) for n in SHIFTS[1:]]


def with_swapped(near):
    return [m for one in near for m in (one, swap(one))]


def chip_sums(own, other):
    got = swap(other)
    sums = [own[n].astype(F32) + got[n].astype(F32) for n in range(4)]
    return sums[:1] + [one.astype(BF16) for one in sums[1:]]


def send_first(sums):
    here, before, after, far = sums
    half = far.shape[0] // 2
    via = [step_y(far[:half], 1), step_y(far[half:], -1)]
    free = [step_y(after[half:], 1), step_y(before[:half], -1)]
    return via, free


def added(sums, via):
    here, before, after, far = sums
    half = far.shape[0] // 2
    add = lambda a, b: (a.astype(F32) + b.astype(F32)).astype(BF16)
    return [add(after[:half], via[0]), add(before[half:], via[1])]


def send_last(ahead, back):
    return [step_y(ahead, 1), step_y(back, -1)]


def joined(free, late):
    return [
        jnp.concatenate([late[0], free[0]], axis=0),
        jnp.concatenate([free[1], late[1]], axis=0),
    ]


def finish(base, sums, arrived):
    here = sums[0]
    for one in arrived:
        here = here + one.astype(F32)
    return (base + here).astype(BF16)


SHIFTS = (0, 1, -1, 2)


FETCH = (
    ((2, 2), (1, 1), (-1, 0), (2, 1), (1, 0), (2, -1), (2, 0), (0, 2)),
    ((0, 0), (-1, -1), (1, 2), (0, -1), (-1, 2), (0, 1), (1, -1), (-1, 1)),
)
SIDE = 4


def fetch_pairs(offsets):
    return [
        (
            (SIDE * x + z) * 8 + m,
            (SIDE * ((x + offsets[m][0]) % SIDE) + (z + offsets[m][1]) % SIDE) * 8 + m,
        )
        for x in range(SIDE)
        for z in range(SIDE)
        for m in range(8)
    ]


def fetched_heads():
    table = np.zeros((16, 8, 16), np.int32)
    for x in range(SIDE):
        for z in range(SIDE):
            for own in range(8):
                y, c = own // 2, own % 2
                members = [2 * ((y - d) % SIDE) + e for e in (c, 1 - c) for d in SHIFTS]
                table[SIDE * x + z, own] = [
                    SIDE * ((x - f[m][0]) % SIDE) + (z - f[m][1]) % SIDE
                    for m in members
                    for f in FETCH
                ]
    return table


def gather_projection(out_proj, sent):
    first, second = [lax.ppermute(out_proj, ("seq", "exp"), fetch_pairs(f)) for f in FETCH]
    first, second, sent = lax.optimization_barrier((first, second, sent))
    up, down = [step_y(w, 1) for w in (first, second)], [step_y(w, -1) for w in (first, second)]
    near = [first, second] + up + down + [step_y(up[0], 1), step_y(down[1], -1)]
    heads = lax.dynamic_slice(
        jnp.asarray(fetched_heads()),
        (lax.axis_index("seq"), lax.axis_index("exp"), 0),
        (1, 1, 16),
    ).reshape(16)
    return heads, near + [swap(w) for w in near], sent


def shards(
    stream,
    stream_tangent,
    query_rows,
    key_rows,
    value_rows,
    query_tangent,
    key_tangent,
    value_tangent,
    out_proj,
    norm_gain,
    gate_weight,
    up_weight,
    down_weight,
    route_ids,
    route_weights,
):
    tok_dev = stream.shape[1]
    own = lax.axis_index("exp")

    sent = pack(
        [
            query_rows[0],
            key_rows[0],
            value_rows[0],
            query_tangent[0],
            key_tangent[0],
            value_tangent[0],
        ]
    )
    heads, weights, sent = gather_projection(out_proj, sent)
    received = lax.all_to_all(sent, "seq", split_axis=0, concat_axis=0, tiled=True)
    attended, attended_tangent = attend(received)
    back = lax.all_to_all(attended, "seq", split_axis=0, concat_axis=0, tiled=True)

    experts_total = lax.axis_size("exp")
    flat_ids = route_ids.reshape(-1)
    onehot = (flat_ids[:, None] == jnp.arange(experts_total, dtype=jnp.int32)[None, :]).astype(
        jnp.int32
    )
    rank_in = jnp.sum((jnp.cumsum(onehot, axis=0) - onehot) * onehot, axis=1)
    rank_in = rank_in.reshape(tok_dev, -1)
    ids = route_ids[0]
    fields = []
    for n in range(2):
        fields += [ids[:, n].astype(BF16), rank_in[:, n].astype(BF16), route_weights[0, :, n]]
    info = jnp.concatenate(
        [jnp.stack(fields), jnp.zeros((INFO - len(fields), tok_dev), BF16)], axis=0
    )

    gain = norm_gain.reshape(1, -1)
    hidden, message = project(True, heads, back, weights, stream[0], gain, info)
    back = lax.all_to_all(attended_tangent, "seq", split_axis=0, concat_axis=0, tiled=True)
    hidden_tangent, message_tangent = project(
        False, heads, back, weights, stream_tangent[0], gain, hidden
    )

    me = own.astype(jnp.int32).reshape(1)
    near = spread(message)
    *mats, loaded = load_expert(gate_weight[0], up_weight[0], down_weight[0])
    near, loaded = lax.optimization_barrier((near, loaded))
    near_tangent = spread(message_tangent)
    part, part_other, *more = expert(True, me, with_swapped(near), mats, [], loaded)
    part_other, near_tangent = lax.optimization_barrier((part_other, near_tangent))
    tokens_tangent = with_swapped(near_tangent)
    sums = chip_sums(part, part_other)
    tokens_tangent, sums = lax.optimization_barrier((tokens_tangent, sums))
    via, free = send_first(sums)
    dpart, dpart_other = expert(False, me, tokens_tangent, mats, more)
    dpart_other, via, free = lax.optimization_barrier((dpart_other, via, free))
    late = send_last(*added(sums, via))
    dsums = chip_sums(dpart, dpart_other)
    dvia, dfree = send_first(dsums)
    dlast = added(dsums, dvia)
    dlast, late = lax.optimization_barrier((dlast, late))
    layer_out = finish(hidden, sums, joined(free, late))
    layer_tangent = finish(hidden_tangent, dsums, joined(dfree, send_last(*dlast)))
    return (layer_out[None], layer_tangent[None])


def solution(mesh):
    rows = P("exp", "seq", None)
    in_specs = (rows,) * 8 + (
        P("seq", None),
        P(),
        P("exp", None, None),
        P("exp", None, None),
        P("exp", None, None),
        rows,
        rows,
    )
    return jax.shard_map(
        shards, mesh=mesh, in_specs=in_specs, out_specs=(rows, rows), check_vma=False
    )
```
